512 devices in a mesh: phase: 4 (over x), blk: 32 (over z, core), rep: 4 (over y).
Axes of the slice: x: 4, y: 4, z: 16, core: 2. Of those that a mesh axis runs over, the one named last changes fastest.
Arguments:
- descriptors: float32 [4, 32, 32768], P(None, None, ('blk', 'rep')), may hold values from -6 to 6
- positions: float32 [4, 3, 32768], P(None, None, 'blk'), as said below
- elements: int32 [4, 32768], P(None, 'blk'), may hold values from 0 to 1
- fragments: int32 [4, 32768], P(None, ('blk', 'rep')), may hold values from 0 to 3, as said below
- neg_input: float32 [2, 15, 32], replicated, may hold values from -1 to 1
- neg_bias: float32 [2, 15], replicated, may hold values from -3 to 3
- neg_hidden: float32 [2, 15, 15], replicated, may hold values from -1.5 to 1.5
- neg_output: float32 [2, 15], replicated, may hold values from -2.4 to 2.4
- short_input: float32 [2, 15, 32], replicated, may hold values from -1 to 1
- short_charge: float32 [2, 15], replicated, may hold values from -12 to 12
- short_bias: float32 [2, 15], replicated, may hold values from -3 to 3
- short_hidden: float32 [2, 15, 15], replicated, may hold values from -1.5 to 1.5
- short_output: float32 [2, 15], replicated, may hold values from -2.4 to 2.4
- widths: float32 [2], replicated, may hold values from 0.8 to 1.6
- hardness: float32 [2], replicated, may hold values from 0.5 to 2
Outputs:
- charges: float32 [4, 32768], P('phase', ('blk', 'rep'))
- energies: float32 [4, 32768], P('phase', ('blk', 'rep'))
The draws below stay inside these ranges and needn't reach their ends.
Inputs may be any that keep to these rules, and one draw needn't show every extreme that they name: `positions`: each atom lies within 0.7 in each coordinate of its own site of a box lattice of spacing 2, one atom a site, so any two atoms are at least 0.6 apart. `fragments`: each molecule holds exactly 8192 atoms of a frame.
All inputs are finite; a program needn't handle non-finite values.
Results may differ from the reference program's by a relative error of at most 0.00035.
Values sent between devices are 32-bit elements; how exact they have to be, the bound alone decides.
No kernel may reach another device: no remote copies, remote signals or barrier semaphores. Data moves between devices by JAX's collectives and lax.ppermute only.
A program may use at most 64 MiB of HBM per device.

```python
import math
import jax
import jax.numpy as jnp
from jax import lax

G = 32
HID = 15
ELEMS = 2
ITERS = 4
FRAGS = 4
ATOMS = 32768
FRAMES = 4


spacing = 2.0


def lattice_sites(key):
    frame_keys = jax.random.split(key, FRAMES)
    return jax.vmap(lambda frame_key: jax.random.permutation(frame_key, ATOMS))(frame_keys).astype(jnp.int32)


def draw_positions(key, part):
    sites = lattice_sites(key)
    key = jax.random.fold_in(key, 11)
    levels = ATOMS.bit_length() - 1
    bits_x = (levels + 2) // 3
    bits_y = (levels - bits_x + 1) // 2
    size_x = 2 ** bits_x
    size_y = 2 ** bits_y
    size_z = ATOMS // (size_x * size_y)
    index_x = (sites % size_x).astype(jnp.float32) - (size_x - 1) / 2.0
    index_y = (sites // size_x % size_y).astype(jnp.float32) - (size_y - 1) / 2.0
    index_z = (sites // (size_x * size_y)).astype(jnp.float32) - (size_z - 1) / 2.0
    lattice = jnp.stack([index_x, index_y, index_z], axis=1)
    jitter = jnp.clip(0.15 * jax.random.normal(key, lattice.shape, jnp.float32), -0.35, 0.35)
    return (spacing * (lattice + jitter)).astype(jnp.float32)


def draw_fragments(key, part):
    sites = lattice_sites(key)
    return (sites * FRAGS // ATOMS).astype(jnp.int32)


def with_ends(values, key, least, largest):
    longest = values.shape.index(max(values.shape))
    spots = []
    for shift in (0, 1):
        where = [jax.random.randint(jax.random.fold_in(key, axis), (), 0, length) for axis, length in enumerate(values.shape)]
        where[longest] = (where[longest] + shift) % values.shape[longest]
        spots.append(tuple(where))
    return values.at[spots[0]].set(least).at[spots[1]].set(largest)


def steps_of(key, dims, cuts, least, largest):
    factor_of = 1.0
    for dim, blocks in cuts:
        steps = jax.random.uniform(jax.random.fold_in(jax.random.fold_in(key, 6), dim), (blocks,), jnp.float32, least / len(cuts), largest / len(cuts))
        factor_of = factor_of * jnp.repeat(jnp.exp(steps), dims[dim] // blocks).reshape((-1,) + (1,) * (len(dims) - 1 - dim))
    return factor_of


def centred(key, shape, width, reach, cuts=(), held_as=jnp.bfloat16):
    entries = width * jax.random.normal(key, shape, jnp.float32)
    if cuts:
        entries = entries * steps_of(key, shape, cuts, -0.22, 0.18)
    return jnp.clip(entries, -reach, reach).astype(held_as)


def setup_inputs(seed: int = 0) -> dict:
    splits = jax.random.split(jax.random.key(seed), 16)
    descriptors = centred(splits[0], (FRAMES, G, ATOMS), 1.0, 6.0, ((2, 128),), jnp.float32)
    positions = draw_positions(jax.random.fold_in(splits[15], 71), 0)
    elements = with_ends(jax.random.randint(splits[2], (FRAMES, ATOMS), 0, ELEMS), jax.random.fold_in(splits[2], 1), 0, ELEMS - 1).astype(jnp.int32)
    fragments = draw_fragments(jax.random.fold_in(splits[15], 71), 0)
    neg_input = centred(splits[4], (ELEMS, HID, G), G ** -0.5, 1.0, (), jnp.float32)
    neg_bias = centred(splits[5], (ELEMS, HID), 0.5, 3.0, (), jnp.float32)
    neg_hidden = centred(splits[6], (ELEMS, HID, HID), HID ** -0.5, 1.5, (), jnp.float32)
    neg_output = centred(splits[7], (ELEMS, HID), 0.4, 2.4, (), jnp.float32)
    short_input = centred(splits[8], (ELEMS, HID, G), G ** -0.5, 1.0, (), jnp.float32)
    short_charge = centred(splits[9], (ELEMS, HID), 2.0, 12.0, (), jnp.float32)
    short_bias = centred(splits[10], (ELEMS, HID), 0.5, 3.0, (), jnp.float32)
    short_hidden = centred(splits[11], (ELEMS, HID, HID), HID ** -0.5, 1.5, (), jnp.float32)
    short_output = centred(splits[12], (ELEMS, HID), 0.4, 2.4, (), jnp.float32)
    widths = jnp.clip(jnp.exp(jax.random.uniform(splits[13], (ELEMS,), jnp.float32, math.log(0.8), math.log(1.6))), 0.8, 1.6)
    hardness = jnp.clip(jnp.exp(jax.random.uniform(splits[14], (ELEMS,), jnp.float32, math.log(0.5), math.log(2.0))), 0.5, 2.0)
    return dict(descriptors=descriptors, positions=positions, elements=elements, fragments=fragments, neg_input=neg_input, neg_bias=neg_bias, neg_hidden=neg_hidden, neg_output=neg_output, short_input=short_input, short_charge=short_charge, short_bias=short_bias, short_hidden=short_hidden, short_output=short_output, widths=widths, hardness=hardness)


highest = lax.Precision.HIGHEST
inv_sqrt_pi = 0.5641895835477563

def network(layer_in, layer_bias, layer_mid, layer_out, features, addition):
    hidden_one = jnp.einsum('ehg,gn->ehn', layer_in, features, precision=highest) + layer_bias[:, :, None] + addition
    hidden_one = jnp.tanh(hidden_one)
    hidden_two = jnp.tanh(jnp.einsum('ehk,ekn->ehn', layer_mid, hidden_one, precision=highest))
    return jnp.einsum('eh,ehn->en', layer_out, hidden_two, precision=highest)

def select_kind(values, element_ids):
    classes = jnp.arange(values.shape[0], dtype=jnp.int32)[:, None]
    return lax.optimization_barrier(jnp.sum(jnp.where(element_ids[None, :] == classes, values, jnp.float32(0.0)), axis=0))

def pair_field(targets, sources, source_values, target_ids, source_ids):
    delta_x = targets[0][:, None] - sources[0][None, :]
    delta_y = targets[1][:, None] - sources[1][None, :]
    delta_z = targets[2][:, None] - sources[2][None, :]
    squared = delta_x * delta_x + delta_y * delta_y + delta_z * delta_z
    itself = target_ids[:, None] == source_ids[None, :]
    distance = jnp.sqrt(jnp.where(itself, 1.0, squared))
    inverse_width = lax.rsqrt(targets[3][:, None] + sources[3][None, :])
    kernel = jnp.where(itself, 0.0, lax.erf(distance * inverse_width) / distance)
    return lax.optimization_barrier(jnp.sum(kernel * source_values[None, :], axis=1))

def project(vector, onehot, members):
    sums = jnp.dot(onehot, vector, precision=highest)
    return vector - jnp.dot(sums / members, onehot, precision=highest)

def reference(descriptors, positions, elements, fragments, neg_input, neg_bias, neg_hidden, neg_output, short_input, short_charge, short_bias, short_hidden, short_output, widths, hardness):
    classes = jnp.arange(FRAGS, dtype=jnp.int32)[:, None]
    members = jnp.float32(ATOMS // FRAGS)
    block_rows = min(ATOMS, 512)

    def one_frame(frame_data):
        features, coords_frame, element_ids, groups = frame_data
        onehot = (groups[None, :] == classes).astype(jnp.float32)
        width_atom = select_kind(jnp.broadcast_to(widths[:, None], (ELEMS, ATOMS)), element_ids)
        geometry = jnp.concatenate([coords_frame, (width_atom * width_atom)[None, :]], axis=0)
        diagonal = select_kind(jnp.broadcast_to(hardness[:, None], (ELEMS, ATOMS)), element_ids) + inv_sqrt_pi / width_atom
        atom_ids = jnp.arange(ATOMS, dtype=jnp.int32)
        tiled_geometry = geometry.reshape(4, ATOMS // block_rows, block_rows).transpose(1, 0, 2)
        tiled_ids = atom_ids.reshape(ATOMS // block_rows, block_rows)

        def apply_matrix(vector):
            field = lax.map(lambda tile_data: pair_field(tile_data[0], geometry, vector, tile_data[1], atom_ids), (tiled_geometry, tiled_ids))
            return diagonal * vector + field.reshape(ATOMS)
        electroneg = select_kind(network(neg_input, neg_bias, neg_hidden, neg_output, features, 0.0), element_ids)
        residual = project(-electroneg, onehot, members)
        direction = residual
        charges = jnp.zeros_like(electroneg)
        norm_now = jnp.sum(residual * residual)
        for iteration in range(ITERS):
            applied = apply_matrix(direction)
            step_size = norm_now / jnp.sum(direction * applied)
            charges = charges + step_size * direction
            residual = residual - step_size * project(applied, onehot, members)
            norm_next = jnp.sum(residual * residual)
            direction = residual + norm_next / norm_now * direction
            norm_now = norm_next
        addition = short_charge[:, :, None] * charges[None, None, :]
        energies = select_kind(network(short_input, short_bias, short_hidden, short_output, features, addition), element_ids)
        return (charges, energies)
    charges, energies = lax.map(one_frame, (descriptors, positions, elements, fragments))
    return (charges, energies)
```

```python
import functools

import jax
import jax.numpy as jnp
from jax import lax
from jax.experimental import pallas as pl
from jax.experimental.pallas import tpu as pltpu
from jax.sharding import Mesh
from jax.sharding import PartitionSpec as P


FRAGS = 4
ELEMS = 2
LANES = 128
OWN = 256
REPS = 4
BLKS = 32
GROUPS = OWN // 8
PIECE = BLKS * 2
ROWS = REPS * PIECE
WINDOW = 16

highest = lax.Precision.HIGHEST
inv_sqrt_pi = 0.5641895835477563
float32 = jnp.float32
VMEM = pl.BlockSpec(memory_space=pltpu.VMEM)
SMEM = pl.BlockSpec(memory_space=pltpu.SMEM)
PARAMS = pltpu.CompilerParams(vmem_limit_bytes=12 * 2**20)


def shaped(*shape):
    return jax.ShapeDtypeStruct(shape, float32)


def eye(size):
    return lax.broadcasted_iota(jnp.int32, (size, size), 0) == lax.broadcasted_iota(jnp.int32, (size, size), 1)


def as_column(row):
    return jnp.sum(jnp.where(eye(row.shape[1]), row, 0.0), axis=1, keepdims=True)


def as_rows(row):
    return jnp.broadcast_to(row, (LANES, LANES)).T


def total_of(values):
    return jnp.sum(jnp.sum(values, axis=0, keepdims=True), axis=1, keepdims=True)


def network(layer_in, layer_bias, layer_mid, layer_out, features, addition):
    outs = []
    for kind in range(ELEMS):
        hidden_one = jnp.dot(layer_in[kind], features, precision=highest, preferred_element_type=float32)
        hidden_one = hidden_one + as_column(layer_bias[kind : kind + 1, :])
        if addition is not None:
            weights, charges = addition
            hidden_one = hidden_one + as_column(weights[kind : kind + 1, :]) * charges
        hidden_one = jnp.tanh(hidden_one)
        hidden_two = jnp.tanh(jnp.dot(layer_mid[kind], hidden_one, precision=highest, preferred_element_type=float32))
        outs.append(jnp.sum(as_column(layer_out[kind : kind + 1, :]) * hidden_two, axis=0, keepdims=True))
    return outs


def prepare_kernel(place, features, coords, kinds, groups, layer_in, layer_bias, layer_mid, layer_out, message):
    frames = features.shape[0]
    own = pl.ds(pl.multiple_of(place[0] * OWN, OWN), OWN)
    wide = jnp.concatenate([features[frame] for frame in range(frames)], axis=1)
    first, second = network(layer_in, layer_bias, layer_mid, layer_out, wide, None)
    chosen = kinds[:, own]
    for frame in range(frames):
        span = slice(frame * OWN, frame * OWN + OWN)
        kind = chosen[frame : frame + 1, :]
        electroneg = jnp.where(kind == 1, second[:, span], first[:, span])
        spot = coords[frame, :, own]
        values = [spot[0:1], spot[1:2], spot[2:3], kind.astype(float32)]
        values += [electroneg, groups[frame : frame + 1, :].astype(float32)]
        for pair in range(3):
            one, two = values[2 * pair], values[2 * pair + 1]
            block = jnp.concatenate([one[:, :LANES], one[:, LANES:], two[:, :LANES], two[:, LANES:]], axis=0)
            for target in range(BLKS // frames):
                message[frame * (BLKS // frames) + target, pair] = block


def fill_rows(atoms, own_block, widths, rows):
    narrow, broad = widths[0], widths[1]
    for half in range(2):
        span = slice(half * LANES, half * LANES + LANES)
        for axis, (pair, line) in enumerate(((0, 0), (0, 2), (1, 0))):
            rows[axis, span] = as_rows(atoms[own_block, pair, line + half : line + half + 1, :])
        kind = as_rows(atoms[own_block, 1, 2 + half : 3 + half, :])
        width = jnp.where(kind > 0.5, broad, narrow)
        rows[3, span] = lax.rsqrt(width * width + narrow * narrow)
        rows[4, span] = lax.rsqrt(width * width + broad * broad)


def build_piece(atoms, rows, piece):
    def one_block(block, carry):
        for half in range(2):
            x, y, z, kind = (
                jnp.broadcast_to(atoms[block, pair, line + half : line + half + 1, :], (8, LANES))
                for pair, line in ((0, 0), (0, 2), (1, 0), (1, 2))
            )
            second = kind > 0.5
            for group in range(GROUPS):
                span = slice(group * 8, group * 8 + 8)
                delta_x = rows[0, span] - x
                delta_y = rows[1, span] - y
                delta_z = rows[2, span] - z
                squared = delta_x * delta_x + delta_y * delta_y + delta_z * delta_z
                inverse = lax.rsqrt(squared)
                scale = jnp.where(second, rows[4, span], rows[3, span])
                piece[2 * block + half, span, :] = lax.erf(squared * inverse * scale) * inverse
        return carry

    lax.fori_loop(0, BLKS, one_block, 0)


def build_own_kernel(place, atoms, widths, hardness, piece, rows):
    own_block = place[1]
    fill_rows(atoms, own_block, widths, rows)
    build_piece(atoms, rows, piece)
    for half in range(2):
        span = slice(half * LANES, half * LANES + LANES)
        second = as_rows(atoms[own_block, 1, 2 + half : 3 + half, :]) > 0.5
        diagonal = jnp.where(second, hardness[1], hardness[0]) + inv_sqrt_pi / jnp.where(second, widths[1], widths[0])
        tile = piece[2 * own_block + half, span, :]
        piece[2 * own_block + half, span, :] = jnp.where(eye(LANES), diagonal, tile)


def apply_rows(pieces, direction, rep):
    sums = tuple(jnp.zeros((8, LANES), float32) for _ in range(GROUPS))
    for turn, piece in enumerate(pieces):
        first = lax.rem(rep + turn, REPS) * PIECE

        def one_line(line, sums):
            values = jnp.broadcast_to(direction[pl.ds(first + line, 1), :], (8, LANES))
            return tuple(
                sums[group] + piece[line, group * 8 : group * 8 + 8, :] * values for group in range(GROUPS)
            )

        sums = lax.fori_loop(0, PIECE, one_line, sums, unroll=8)
    half = GROUPS // 2
    return [
        jnp.sum(jnp.concatenate(sums[part * half : part * half + half], axis=0).T, axis=0, keepdims=True)
        for part in range(2)
    ]


def write_message(image, message):
    block = jnp.concatenate(image * 4, axis=0)
    for line in range(ROWS // 8):
        message[line * 8 : line * 8 + 8, :] = block


def project(vector, groups):
    members = ROWS * LANES // FRAGS
    taken = jnp.zeros_like(vector)
    for group in range(FRAGS):
        inside = groups == float(group)
        mean = total_of(jnp.where(inside, vector, 0.0)) / members
        taken = jnp.where(inside, mean, taken)
    return vector - taken


def first_kernel(place, atoms, widths, own_piece, piece_1, piece_2, piece_3, message, residual, groups, norm, rows):
    rep = place[0]
    fill_rows(atoms.at[rep], place[1], widths, rows)
    for turn, piece in ((1, piece_1), (2, piece_2), (3, piece_3)):
        build_piece(atoms.at[lax.rem(rep + turn, REPS)], rows, piece)
    for part in range(REPS):
        for block in range(BLKS):
            line = part * PIECE + block * 2
            residual[line : line + 2, :] = atoms[part, block, 2, 0:2, :]
            groups[line : line + 2, :] = atoms[part, block, 2, 2:4, :]
    start = -project(residual[...], groups[...])
    residual[...] = start
    norm[...] = jnp.broadcast_to(total_of(start * start), norm.shape)
    write_message(apply_rows((own_piece, piece_1, piece_2, piece_3), residual, rep), message)


def update(image, residual, direction, charges, groups, norm, residual_out, direction_out, charges_out):
    norm_now = norm[0:1, 0:1]
    along, whole = direction[...], image[...]
    step = norm_now / total_of(along * whole)
    charges_out[...] = step * along if charges is None else charges[...] + step * along
    left = residual[...] - step * project(whole, groups[...])
    residual_out[...] = left
    norm_next = total_of(left * left)
    direction_out[...] = left + norm_next / norm_now * along
    return norm_next


def iterate_kernel(*refs, begun):
    place, image, residual, direction = refs[:4]
    charges = refs[4] if begun else None
    groups, norm, *pieces = refs[4 + begun : 10 + begun]
    message, residual_out, direction_out, charges_out, norm_out = refs[10 + begun :]
    norm_next = update(
        image, residual, direction, charges, groups, norm, residual_out, direction_out, charges_out
    )
    norm_out[...] = jnp.broadcast_to(norm_next, norm_out.shape)
    write_message(apply_rows(pieces, direction_out, place[0]), message)


def last_kernel(
    place, image, residual, direction, charges, groups, norm, own, piece_1, piece_2, piece_3, share, message, *scratch
):
    residual_out, direction_out, charges_out = scratch
    rep = place[0]
    norm_next = update(
        image, residual, direction, charges, groups, norm, residual_out, direction_out, charges_out
    )
    applied = apply_rows((own, piece_1, piece_2, piece_3), direction_out, rep)
    line = rep * PIECE + place[1] * 2
    part = applied[0] * direction_out[pl.ds(line, 1), :] + applied[1] * direction_out[pl.ds(line + 1, 1), :]
    share[...] = jnp.broadcast_to(jnp.sum(part, axis=1, keepdims=True) / norm_next, share.shape)
    lines = pl.ds(lax.rem(rep, 2), ROWS // 2, stride=2)
    message[...] = jnp.where(rep < 2, charges_out[lines, :], direction_out[lines, :])


def signal_lane(window):
    return lax.rem(window + 1, LANES // WINDOW) * WINDOW


def join_kernel(place, shares, message, out):
    total = total_of(shares[:, 0:1])
    lane = lax.broadcasted_iota(jnp.int32, message.shape, 1)
    out[...] = jnp.where(lane == signal_lane(place[2]), total, message[...])


def finish_kernel(
    place, parts, features, kinds, layer_in, layer_charge, layer_bias, layer_mid, layer_out, charges_out, energies_out
):
    frame = place[3]
    windows = LANES // WINDOW
    lane = lax.broadcasted_iota(jnp.int32, (windows, LANES), 1)
    window = lax.broadcasted_iota(jnp.int32, (windows, LANES), 0)
    inside = lane // WINDOW == window
    marked = lane == signal_lane(window)
    lines = []
    inverse = jnp.zeros((1, 1), float32)
    for rep in range(REPS):
        block = parts[pl.ds(pl.multiple_of(rep * BLKS + frame * windows, windows), windows), :]
        lines.append(jnp.sum(jnp.where(inside, block, 0.0), axis=0, keepdims=True))
        inverse = inverse + total_of(jnp.where(marked, block, 0.0))
    step = 1.0 / inverse
    charges = jnp.concatenate([lines[0] + step * lines[2], lines[1] + step * lines[3]], axis=1)
    charges_out[...] = charges
    first, second = network(layer_in, layer_bias, layer_mid, layer_out, features[frame], (layer_charge, charges))
    kind = kinds[pl.ds(frame, 1), pl.ds(pl.multiple_of(place[0] * OWN, OWN), OWN)]
    energies_out[...] = jnp.where(kind == 1, second, first)


def call(kernel, outs, name, scratch=(), flops=0):
    def run(place, *args):
        args = [place] + list(args)
        specs = [SMEM if arg.ndim == 1 else VMEM for arg in args]
        many = isinstance(outs, list)
        return pl.pallas_call(
            kernel,
            out_shape=outs,
            in_specs=specs,
            out_specs=[VMEM] * len(outs) if many else VMEM,
            scratch_shapes=list(scratch),
            compiler_params=PARAMS,
            cost_estimate=pl.CostEstimate(flops=flops, bytes_accessed=0, transcendentals=0) if flops else None,
            name=name,
        )(*args)

    return run


def on_device(
    descriptors,
    positions,
    elements,
    fragments,
    neg_input,
    neg_bias,
    neg_hidden,
    neg_output,
    short_input,
    short_charge,
    short_bias,
    short_hidden,
    short_output,
    widths,
    hardness,
):
    rep = lax.axis_index("rep")
    window = lax.axis_index("zr") * 2 + lax.axis_index("core")
    phase = lax.axis_index("phase")
    place = jnp.stack([rep, phase * 8 + window, window, phase]).astype(jnp.int32)
    block_axes = ("zq", "zr", "core")
    cube_axes = ("rep", "phase", "zr", "core")
    column_axes = ("rep", "zq", "zr", "core")
    piece = pltpu.VMEM((PIECE, OWN, LANES), float32)
    whole = shaped(ROWS, LANES)
    small = shaped(8, LANES)
    rows = pltpu.VMEM((5, OWN, LANES), float32)

    def exchange(message):
        sent = message.reshape(ROWS // 2, 2, LANES)
        return lax.all_to_all(sent, cube_axes, 0, 0).reshape(ROWS, LANES)

    def kept(pieces):
        return [pltpu.with_memory_space_constraint(one, pltpu.VMEM) for one in pieces]

    message = call(prepare_kernel, shaped(BLKS, 3, 4, LANES), "prepare")(
        place, descriptors, positions, elements, fragments, neg_input, neg_bias, neg_hidden, neg_output
    )
    atoms_own = lax.all_to_all(message, block_axes, 0, 0)
    atoms = lax.all_to_all(jnp.broadcast_to(atoms_own[None], (REPS,) + atoms_own.shape), "rep", 0, 0)
    piece_0 = call(build_own_kernel, piece, "build_own", [rows], flops=10**9)(place, atoms_own, widths, hardness)
    piece_1, piece_2, piece_3, message, residual, groups, norm = call(
        first_kernel, [piece, piece, piece, whole, whole, whole, small], "build_rest_and_begin", [rows]
    )(place, atoms, widths, *kept([piece_0]))
    pieces = [piece_0, piece_1, piece_2, piece_3]
    message, residual, direction, charges, norm = call(
        functools.partial(iterate_kernel, begun=0), [whole, whole, whole, whole, small], "iterate"
    )(place, exchange(message), residual, residual, groups, norm, *kept(pieces))
    message, residual, direction, charges, norm = call(
        functools.partial(iterate_kernel, begun=1), [whole, whole, whole, whole, small], "iterate"
    )(place, exchange(message), residual, direction, charges, groups, norm, *kept(pieces))
    share, message = call(
        last_kernel, [shaped(4, LANES), shaped(ROWS // 2, LANES)], "last", [pltpu.VMEM((ROWS, LANES), float32)] * 3
    )(place, exchange(message), residual, direction, charges, groups, norm, *kept(pieces))
    shares = lax.all_to_all(share.reshape(4, 1, LANES), "phase", 0, 0).reshape(4, LANES)
    message = call(join_kernel, shaped(ROWS // 2, LANES), "join")(place, shares, message)
    parts = lax.all_to_all(message.reshape(ROWS // 2, 1, LANES), column_axes, 0, 0).reshape(ROWS // 2, LANES)
    return call(finish_kernel, [shaped(1, OWN), shaped(1, OWN)], "finish")(
        place,
        parts,
        descriptors,
        elements,
        short_input,
        short_charge,
        short_bias,
        short_hidden,
        short_output,
    )


def solution(mesh):
    split = Mesh(mesh.devices.reshape(4, 4, 4, 2, 4), ("phase", "zq", "zr", "core", "rep"))
    block_axes = ("zq", "zr", "core")
    return jax.shard_map(
        on_device,
        mesh=split,
        in_specs=(
            P(None, None, block_axes + ("rep",)),
            P(None, None, block_axes),
            P(None, block_axes),
            P(None, block_axes + ("rep",)),
        )
        + (P(),) * 11,
        out_specs=(P("phase", block_axes + ("rep",)), P("phase", block_axes + ("rep",))),
        check_vma=False,
    )
```

```python
import functools

import jax
import jax.numpy as jnp
from jax import lax
from jax.experimental import pallas as pl
from jax.experimental.pallas import tpu as pltpu
from jax.sharding import Mesh
from jax.sharding import PartitionSpec as P


FRAGS = 4
ELEMS = 2
LANES = 128
OWN = 256
REPS = 4
BLKS = 32
GROUPS = OWN // 8
PIECE = BLKS * 2
ROWS = REPS * PIECE
WINDOW = 64

highest = lax.Precision.HIGHEST
inv_sqrt_pi = 0.5641895835477563
float32 = jnp.float32
VMEM = pl.BlockSpec(memory_space=pltpu.VMEM)
SMEM = pl.BlockSpec(memory_space=pltpu.SMEM)
PARAMS = pltpu.CompilerParams(vmem_limit_bytes=12 * 2**20)


def shaped(*shape):
    return jax.ShapeDtypeStruct(shape, float32)


def eye(size):
    return lax.broadcasted_iota(jnp.int32, (size, size), 0) == lax.broadcasted_iota(jnp.int32, (size, size), 1)


def as_column(row):
    return jnp.sum(jnp.where(eye(row.shape[1]), row, 0.0), axis=1, keepdims=True)


def as_rows(row):
    return jnp.broadcast_to(row, (LANES, LANES)).T


def total_of(values):
    return jnp.sum(jnp.sum(values, axis=0, keepdims=True), axis=1, keepdims=True)


def last_layers(layer_mid, layer_out, hidden_one, kind):
    hidden_two = jnp.dot(layer_mid[:, kind, :], hidden_one, precision=highest, preferred_element_type=float32)
    return jnp.sum(as_column(layer_out[kind : kind + 1, :]) * jnp.tanh(hidden_two), axis=0, keepdims=True)


def network(layer_in, layer_bias, layer_mid, layer_out, features):
    outs = []
    for kind in range(ELEMS):
        hidden_one = jnp.dot(layer_in[:, kind, :], features, precision=highest, preferred_element_type=float32)
        hidden_one = jnp.tanh(hidden_one + as_column(layer_bias[kind : kind + 1, :]))
        outs.append(last_layers(layer_mid, layer_out, hidden_one, kind))
    return outs


def place_of():
    window = lax.axis_index("zr") * 2 + lax.axis_index("core")
    return lax.axis_index("rep"), lax.axis_index("phase") * 8 + window, window


def prepare_kernel(*refs):
    given, (message, constants), held, arrived = refs[:10], refs[10:12], refs[12:22], refs[22]
    own = pl.ds(pl.multiple_of(lax.axis_index("rep") * OWN, OWN), OWN)
    copies = []
    for index, (source, target) in enumerate(zip(given, held)):
        source = source.at[:, :, own] if index == 1 else source.at[:, own] if index == 2 else source
        copies.append(pltpu.make_async_copy(source, target, arrived.at[index]))
        copies[-1].start()
    for copy in copies:
        copy.wait()
    features, coords, kinds, groups, layer_in, layer_bias, layer_mid, layer_out, widths, hardness = held
    for line, source in enumerate((widths, hardness)):
        for kind in range(ELEMS):
            row = jnp.broadcast_to(source[0:1, kind : kind + 1], (1, LANES))
            constants[2 * line + kind : 2 * line + kind + 1, :] = row
    frames = features.shape[0]
    wide = jnp.concatenate([features[frame] for frame in range(frames)], axis=1)
    first, second = network(layer_in, layer_bias, layer_mid, layer_out, wide)
    for frame in range(frames):
        span = slice(frame * OWN, frame * OWN + OWN)
        kind = kinds[frame : frame + 1, :]
        electroneg = jnp.where(kind == 1, second[:, span], first[:, span])
        values = [coords[axis, frame : frame + 1, :] for axis in range(3)]
        values += [kind.astype(float32), electroneg, groups[frame : frame + 1, :].astype(float32)]
        for pair in range(3):
            one, two = values[2 * pair], values[2 * pair + 1]
            block = jnp.concatenate([one[:, :LANES], one[:, LANES:], two[:, :LANES], two[:, LANES:]], axis=0)
            for target in range(BLKS // frames):
                message[frame * (BLKS // frames) + target, pair] = block


def fill_rows(atoms, own_block, constants, rows):
    narrow, broad = constants[0:1, 0:1], constants[1:2, 0:1]
    for half in range(2):
        span = slice(half * LANES, half * LANES + LANES)
        for axis, (pair, line) in enumerate(((0, 0), (0, 2), (1, 0))):
            rows[axis, span] = as_rows(atoms[own_block, pair, line + half : line + half + 1, :])
        kind = as_rows(atoms[own_block, 1, 2 + half : 3 + half, :])
        width = jnp.where(kind > 0.5, broad, narrow)
        rows[3, span] = lax.rsqrt(width * width + narrow * narrow)
        rows[4, span] = lax.rsqrt(width * width + broad * broad)


def build_piece(atoms, rows, piece):
    def one_block(block, carry):
        for half in range(2):
            x, y, z, kind = (
                jnp.broadcast_to(atoms[block, pair, line + half : line + half + 1, :], (8, LANES))
                for pair, line in ((0, 0), (0, 2), (1, 0), (1, 2))
            )
            second = kind > 0.5
            for group in range(GROUPS):
                span = slice(group * 8, group * 8 + 8)
                delta_x = rows[0, span] - x
                delta_y = rows[1, span] - y
                delta_z = rows[2, span] - z
                squared = delta_x * delta_x + delta_y * delta_y + delta_z * delta_z
                inverse = lax.rsqrt(squared)
                scale = jnp.where(second, rows[4, span], rows[3, span])
                piece[2 * block + half, span, :] = lax.erf(squared * inverse * scale) * inverse
        return carry

    lax.fori_loop(0, BLKS, one_block, 0, unroll=2)


def build_own_kernel(atoms, constants, piece, rows):
    _, own_block, _ = place_of()
    fill_rows(atoms, own_block, constants, rows)
    build_piece(atoms, rows, piece)
    width_0, width_1, hardness_0, hardness_1 = (constants[line : line + 1, 0:1] for line in range(4))
    for half in range(2):
        span = slice(half * LANES, half * LANES + LANES)
        second = as_rows(atoms[own_block, 1, 2 + half : 3 + half, :]) > 0.5
        diagonal = jnp.where(second, hardness_1, hardness_0) + inv_sqrt_pi / jnp.where(second, width_1, width_0)
        tile = piece[2 * own_block + half, span, :]
        piece[2 * own_block + half, span, :] = jnp.where(eye(LANES), diagonal, tile)


def apply_rows(pieces, direction, rep):
    sums = tuple(jnp.zeros((8, LANES), float32) for _ in range(GROUPS))
    for turn, piece in enumerate(pieces):
        first = lax.rem(rep + turn, REPS) * PIECE

        def one_line(line, sums):
            values = jnp.broadcast_to(direction[pl.ds(first + line, 1), :], (8, LANES))
            return tuple(
                sums[group] + piece[line, group * 8 : group * 8 + 8, :] * values for group in range(GROUPS)
            )

        sums = lax.fori_loop(0, PIECE, one_line, sums, unroll=8)
    half = GROUPS // 2
    return [
        jnp.sum(jnp.concatenate(sums[part * half : part * half + half], axis=0).T, axis=0, keepdims=True)
        for part in range(2)
    ]


def write_message(image, message):
    block = jnp.concatenate(image * 4, axis=0)
    for line in range(ROWS // 8):
        message[line * 8 : line * 8 + 8, :] = block


def project(vector, groups):
    members = ROWS * LANES // FRAGS
    taken = jnp.zeros_like(vector)
    for group in range(FRAGS):
        inside = groups == float(group)
        mean = total_of(jnp.where(inside, vector, 0.0)) / members
        taken = jnp.where(inside, mean, taken)
    return vector - taken


def first_kernel(*refs):
    parts, (rows, own_piece), pieces = refs[:4], refs[4:6], refs[6:9]
    message, residual, groups, norm = refs[9:]
    rep, _, _ = place_of()
    for part, piece in zip(parts[1:], pieces):
        build_piece(part, rows, piece)
    for turn, part in enumerate(parts):
        first = lax.rem(rep + turn, REPS) * PIECE
        for block in range(BLKS):
            residual[pl.ds(first + block * 2, 2), :] = part[block, 2, 0:2, :]
            groups[pl.ds(first + block * 2, 2), :] = part[block, 2, 2:4, :]
    start = -project(residual[...], groups[...])
    residual[...] = start
    norm[...] = jnp.broadcast_to(total_of(start * start), norm.shape)
    write_message(apply_rows((own_piece, *pieces), residual, rep), message)


def update(image, residual, direction, charges, groups, norm, residual_out, direction_out, charges_out):
    norm_now = norm[0:1, 0:1]
    along, whole = direction[...], image[...]
    step = norm_now / total_of(along * whole)
    charges_out[...] = step * along if charges is None else charges[...] + step * along
    left = residual[...] - step * project(whole, groups[...])
    residual_out[...] = left
    norm_next = total_of(left * left)
    direction_out[...] = left + norm_next / norm_now * along
    return norm_next


def iterate_kernel(*refs, begun):
    image, residual, direction = refs[:3]
    charges = refs[3] if begun else None
    groups, norm, *pieces = refs[3 + begun : 9 + begun]
    message, residual_out, direction_out, charges_out, norm_out = refs[9 + begun :]
    norm_next = update(image, residual, direction, charges, groups, norm, residual_out, direction_out, charges_out)
    norm_out[...] = jnp.broadcast_to(norm_next, norm_out.shape)
    write_message(apply_rows(pieces, direction_out, place_of()[0]), message)


def last_kernel(
    image, residual, direction, charges, groups, norm, own, piece_1, piece_2, piece_3, share, message, *scratch
):
    residual_out, direction_out, charges_out = scratch
    rep, own_block, window = place_of()
    norm_next = update(image, residual, direction, charges, groups, norm, residual_out, direction_out, charges_out)
    applied = apply_rows((own, piece_1, piece_2, piece_3), direction_out, rep)
    line = rep * PIECE + own_block * 2
    part = applied[0] * direction_out[pl.ds(line, 1), :] + applied[1] * direction_out[pl.ds(line + 1, 1), :]
    share[...] = jnp.broadcast_to(jnp.sum(part, axis=1, keepdims=True) / norm_next, share.shape)
    lines = pl.ds(rep * PIECE + lax.rem(window // 2, 2), BLKS, stride=2)
    message[...] = jnp.where(window < 4, charges_out[lines, :], direction_out[lines, :])


def join_kernel(shares, message, out):
    _, _, window = place_of()
    lane = lax.broadcasted_iota(jnp.int32, message.shape, 1)
    out[...] = jnp.where(lane // WINDOW == lax.rem(window, 2), message[...], total_of(shares[:, 0:1]))


def input_layer_kernel(features, layer_in, layer_bias, out):
    frame = lax.axis_index("phase")
    for kind in range(ELEMS):
        product = jnp.dot(layer_in[:, kind, :], features[frame], precision=highest, preferred_element_type=float32)
        out[kind] = product + as_column(layer_bias[kind : kind + 1, :])


def finish_kernel(parts, inputs, kinds, layer_charge, layer_mid, layer_out, charges_out, energies_out):
    frame = lax.axis_index("phase")
    senders = LANES // WINDOW * 4
    block = parts[pl.ds(pl.multiple_of(frame * senders, senders), senders), :]
    lane = lax.broadcasted_iota(jnp.int32, block.shape, 1) // WINDOW
    sender = lax.broadcasted_iota(jnp.int32, block.shape, 0)
    inside = lane == lax.rem(sender, 2)
    lines = [
        jnp.sum(jnp.where(inside & (sender // 2 == line), block, 0.0), axis=0, keepdims=True) for line in range(4)
    ]
    step = LANES - WINDOW
    step = step / total_of(jnp.where(inside, 0.0, block))
    charges = jnp.concatenate([lines[0] + step * lines[2], lines[1] + step * lines[3]], axis=1)
    charges_out[...] = charges
    outs = []
    for kind in range(ELEMS):
        hidden_one = jnp.tanh(inputs[kind] + as_column(layer_charge[kind : kind + 1, :]) * charges)
        outs.append(last_layers(layer_mid, layer_out, hidden_one, kind))
    own = pl.ds(pl.multiple_of(lax.axis_index("rep") * OWN, OWN), OWN)
    energies_out[...] = jnp.where(kinds[pl.ds(frame, 1), own] == 1, outs[1], outs[0])


def call(kernel, outs, name, scratch=(), flops=0, held=VMEM):
    def run(*args):
        many = isinstance(outs, list)
        return pl.pallas_call(
            kernel,
            out_shape=outs,
            in_specs=[held] * len(args),
            out_specs=[VMEM] * len(outs) if many else VMEM,
            scratch_shapes=list(scratch),
            compiler_params=PARAMS,
            cost_estimate=pl.CostEstimate(flops=flops, bytes_accessed=0, transcendentals=0) if flops else None,
            name=name,
        )(*args)

    return run


def on_device(
    descriptors,
    positions,
    elements,
    fragments,
    neg_input,
    neg_bias,
    neg_hidden,
    neg_output,
    short_input,
    short_charge,
    short_bias,
    short_hidden,
    short_output,
    widths,
    hardness,
):
    block_axes = ("zq", "zr", "core")
    cube_axes = ("rep", "phase", "zr", "core")
    piece = pltpu.VMEM((PIECE, OWN, LANES), float32)
    rows = pltpu.VMEM((5, OWN, LANES), float32)
    whole = shaped(ROWS, LANES)
    small = shaped(8, LANES)

    def exchange(message):
        sent = message.reshape(ROWS // 2, 2, LANES)
        return lax.all_to_all(sent, cube_axes, 0, 0).reshape(ROWS, LANES)

    def kept(pieces):
        return [pltpu.with_memory_space_constraint(one, pltpu.VMEM) for one in pieces]

    def turned(layer):
        return jnp.transpose(layer, (1, 0, 2))

    given = [descriptors, turned(positions), elements, fragments, turned(neg_input), neg_bias, turned(neg_hidden)]
    given += [neg_output, widths[None, :], hardness[None, :]]
    held = [pltpu.VMEM(one.shape, one.dtype) for one in given]
    held[1] = pltpu.VMEM((3, elements.shape[0], OWN), float32)
    held[2] = pltpu.VMEM((elements.shape[0], OWN), jnp.int32)
    message, constants = call(
        prepare_kernel,
        [shaped(BLKS, 3, 4, LANES), small],
        "prepare",
        held + [pltpu.SemaphoreType.DMA((len(given),))],
        held=pl.BlockSpec(memory_space=pl.ANY),
    )(*[pltpu.with_memory_space_constraint(one, pltpu.HBM) for one in given])
    atoms_own = lax.all_to_all(message, block_axes, 0, 0)
    parts = [
        lax.ppermute(atoms_own, "rep", [((rep + turn) % REPS, rep) for rep in range(REPS)]) for turn in range(1, REPS)
    ]
    own_piece, row_values = call(build_own_kernel, [piece, rows], "build_own", flops=10**9)(atoms_own, constants)
    *rest, message, residual, groups, norm = call(
        first_kernel, [piece] * 3 + [whole, whole, whole, small], "build_rest_and_begin"
    )(atoms_own, *parts, *kept([row_values, own_piece]))
    pieces = [own_piece] + rest
    message, residual, direction, charges, norm = call(
        functools.partial(iterate_kernel, begun=0), [whole, whole, whole, whole, small], "iterate"
    )(exchange(message), residual, residual, groups, norm, *kept(pieces))
    message, residual, direction, charges, norm = call(
        functools.partial(iterate_kernel, begun=1), [whole, whole, whole, whole, small], "iterate"
    )(exchange(message), residual, direction, charges, groups, norm, *kept(pieces))
    share, message = call(
        last_kernel, [shaped(16, LANES), shaped(BLKS, LANES)], "last", [pltpu.VMEM((ROWS, LANES), float32)] * 3
    )(exchange(message), residual, direction, charges, groups, norm, *kept(pieces))
    shares = lax.all_to_all(share.reshape(16, 1, LANES), ("phase", "rep"), 0, 0).reshape(16, LANES)
    message = call(join_kernel, shaped(BLKS, LANES), "join")(shares, message)
    parts = lax.all_to_all(message.reshape(BLKS, 1, LANES), block_axes, 0, 0).reshape(BLKS, LANES)
    inputs = call(input_layer_kernel, shaped(ELEMS, short_bias.shape[1], OWN), "input_layer", flops=10**7)(
        descriptors, turned(short_input), short_bias
    )
    return call(finish_kernel, [shaped(1, OWN), shaped(1, OWN)], "finish")(
        parts, inputs, elements, short_charge, turned(short_hidden), short_output
    )


def solution(mesh):
    split = Mesh(mesh.devices.reshape(4, 4, 4, 2, 4), ("phase", "zq", "zr", "core", "rep"))
    block_axes = ("zq", "zr", "core")
    return jax.shard_map(
        on_device,
        mesh=split,
        in_specs=(
            P(None, None, block_axes + ("rep",)),
            P(None, None, block_axes),
            P(None, block_axes),
            P(None, block_axes + ("rep",)),
        )
        + (P(),) * 11,
        out_specs=(P("phase", block_axes + ("rep",)), P("phase", block_axes + ("rep",))),
        check_vma=False,
    )
```

```python
import functools

import jax
import jax.numpy as jnp
import numpy as np
from jax import lax
from jax.experimental import pallas as pl
from jax.experimental.pallas import tpu as pltpu
from jax.sharding import Mesh
from jax.sharding import PartitionSpec as P


FRAGS = 4
ELEMS = 2
LANES = 128
OWN = 256
REPS = 4
BLKS = 32
GROUPS = OWN // 8
PIECE = BLKS * 2
ROWS = REPS * PIECE
WINDOW = 64

highest = lax.Precision.HIGHEST
inv_sqrt_pi = 0.5641895835477563
float32 = jnp.float32
VMEM = pl.BlockSpec(memory_space=pltpu.VMEM)
SMEM = pl.BlockSpec(memory_space=pltpu.SMEM)
PARAMS = pltpu.CompilerParams(vmem_limit_bytes=12 * 2**20)


def shaped(*shape):
    return jax.ShapeDtypeStruct(shape, float32)


def eye(size):
    return lax.broadcasted_iota(jnp.int32, (size, size), 0) == lax.broadcasted_iota(jnp.int32, (size, size), 1)


def as_column(row):
    return jnp.sum(jnp.where(eye(row.shape[1]), row, 0.0), axis=1, keepdims=True)


def as_rows(row):
    return jnp.broadcast_to(row, (LANES, LANES)).T


def total_of(values):
    return jnp.sum(jnp.sum(values, axis=0, keepdims=True), axis=1, keepdims=True)


def last_layers(layer_mid, layer_out, hidden_one, kind):
    hidden_two = jnp.dot(layer_mid[:, kind, :], hidden_one, precision=highest, preferred_element_type=float32)
    return jnp.sum(as_column(layer_out[kind : kind + 1, :]) * jnp.tanh(hidden_two), axis=0, keepdims=True)


def network(layer_in, layer_bias, layer_mid, layer_out, features):
    outs = []
    for kind in range(ELEMS):
        hidden_one = jnp.dot(layer_in[:, kind, :], features, precision=highest, preferred_element_type=float32)
        hidden_one = jnp.tanh(hidden_one + as_column(layer_bias[kind : kind + 1, :]))
        outs.append(last_layers(layer_mid, layer_out, hidden_one, kind))
    return outs


def place_of():
    core, spot = lax.axis_index("core"), lax.axis_index("zr")
    turned = jnp.where(lax.axis_index("zq") < 2, 3 - spot, spot)
    return lax.axis_index("rep"), core * 16 + lax.rem(lax.axis_index("phase") + 2, 4) * 4 + turned, core * 4 + spot


def row_of(rep, line):
    return line // 32 * 128 + lax.rem(rep + 2, 4) * 32 + line % 32


def all_devices():
    return np.arange(512).reshape(4, 4, 4, 2, 4)[[2, 3, 0, 1]][..., [2, 3, 0, 1]]


def listed(groups):
    return [[int(device) for device in group] for group in groups]


def cube_groups():
    devices = all_devices()
    devices[:, :2] = devices[:, :2, ::-1].copy()
    return listed(devices.transpose(1, 3, 4, 0, 2).reshape(4, 128))


def block_groups():
    return listed(all_devices()[:, [2, 3, 0, 1]].transpose(0, 4, 3, 1, 2).reshape(16, BLKS))


def layer_groups():
    return listed(all_devices().transpose(1, 2, 3, 0, 4).reshape(BLKS, 16))


def prepare_kernel(*refs):
    given, (message, constants), held, arrived = refs[:10], refs[10:12], refs[12:22], refs[22]
    own = pl.ds(pl.multiple_of(lax.axis_index("rep") * OWN, OWN), OWN)
    copies = []
    for index, (source, target) in enumerate(zip(given, held)):
        source = source.at[:, :, own] if index == 1 else source.at[:, own] if index == 2 else source
        copies.append(pltpu.make_async_copy(source, target, arrived.at[index]))
        copies[-1].start()
    for copy in copies:
        copy.wait()
    features, coords, kinds, groups, layer_in, layer_bias, layer_mid, layer_out, widths, hardness = held
    for line, source in enumerate((widths, hardness)):
        for kind in range(ELEMS):
            row = jnp.broadcast_to(source[0:1, kind : kind + 1], (1, LANES))
            constants[2 * line + kind : 2 * line + kind + 1, :] = row
    frames = features.shape[0]
    wide = jnp.concatenate([features[frame] for frame in range(frames)], axis=1)
    first, second = network(layer_in, layer_bias, layer_mid, layer_out, wide)
    for frame in range(frames):
        span = slice(frame * OWN, frame * OWN + OWN)
        kind = kinds[frame : frame + 1, :]
        electroneg = jnp.where(kind == 1, second[:, span], first[:, span])
        values = [coords[axis, frame : frame + 1, :] for axis in range(3)]
        values += [kind.astype(float32), electroneg, groups[frame : frame + 1, :].astype(float32)]
        for pair in range(3):
            one, two = values[2 * pair], values[2 * pair + 1]
            block = jnp.concatenate([one[:, :LANES], one[:, LANES:], two[:, :LANES], two[:, LANES:]], axis=0)
            for target in range(BLKS // frames):
                message[target // 4 * 16 + (frame + 2) % 4 * 4 + target % 4, pair] = block


def fill_rows(atoms, own_block, constants, rows):
    narrow, broad = constants[0:1, 0:1], constants[1:2, 0:1]
    for half in range(2):
        span = slice(half * LANES, half * LANES + LANES)
        for axis, (pair, line) in enumerate(((0, 0), (0, 2), (1, 0))):
            rows[axis, span] = as_rows(atoms[own_block, pair, line + half : line + half + 1, :])
        kind = as_rows(atoms[own_block, 1, 2 + half : 3 + half, :])
        width = jnp.where(kind > 0.5, broad, narrow)
        rows[3, span] = lax.rsqrt(width * width + narrow * narrow)
        rows[4, span] = lax.rsqrt(width * width + broad * broad)


def build_piece(atoms, rows, piece):
    def one_block(block, carry):
        for half in range(2):
            x, y, z, kind = (
                jnp.broadcast_to(atoms[block, pair, line + half : line + half + 1, :], (8, LANES))
                for pair, line in ((0, 0), (0, 2), (1, 0), (1, 2))
            )
            second = kind > 0.5
            for group in range(GROUPS):
                span = slice(group * 8, group * 8 + 8)
                delta_x = rows[0, span] - x
                delta_y = rows[1, span] - y
                delta_z = rows[2, span] - z
                squared = delta_x * delta_x + delta_y * delta_y + delta_z * delta_z
                inverse = lax.rsqrt(squared)
                scale = jnp.where(second, rows[4, span], rows[3, span])
                piece[2 * block + half, span, :] = lax.erf(squared * inverse * scale) * inverse
        return carry

    lax.fori_loop(0, BLKS, one_block, 0, unroll=2)


def build_own_kernel(atoms, constants, piece, rows):
    _, own_block, _ = place_of()
    fill_rows(atoms, own_block, constants, rows)
    build_piece(atoms, rows, piece)
    width_0, width_1, hardness_0, hardness_1 = (constants[line : line + 1, 0:1] for line in range(4))
    for half in range(2):
        span = slice(half * LANES, half * LANES + LANES)
        second = as_rows(atoms[own_block, 1, 2 + half : 3 + half, :]) > 0.5
        diagonal = jnp.where(second, hardness_1, hardness_0) + inv_sqrt_pi / jnp.where(second, width_1, width_0)
        tile = piece[2 * own_block + half, span, :]
        piece[2 * own_block + half, span, :] = jnp.where(eye(LANES), diagonal, tile)


def apply_rows(pieces, direction, rep):
    sums = tuple(jnp.zeros((8, LANES), float32) for _ in range(GROUPS))
    for turn, piece in enumerate(pieces):
        for core in range(2):
            first = row_of(lax.rem(rep + turn, REPS), core * BLKS)

            def one_line(line, sums, core=core, piece=piece, first=first):
                values = jnp.broadcast_to(direction[pl.ds(first + line, 1), :], (8, LANES))
                here = core * BLKS + line
                return tuple(
                    sums[group] + piece[here, group * 8 : group * 8 + 8, :] * values for group in range(GROUPS)
                )

            sums = lax.fori_loop(0, BLKS, one_line, sums, unroll=8)
    half = GROUPS // 2
    return [
        jnp.sum(jnp.concatenate(sums[part * half : part * half + half], axis=0).T, axis=0, keepdims=True)
        for part in range(2)
    ]


def write_message(image, message):
    block = jnp.concatenate(image * 4, axis=0)
    for line in range(ROWS // 8):
        message[line * 8 : line * 8 + 8, :] = block


def project(vector, groups):
    members = ROWS * LANES // FRAGS
    taken = jnp.zeros_like(vector)
    for group in range(FRAGS):
        inside = groups == float(group)
        mean = total_of(jnp.where(inside, vector, 0.0)) / members
        taken = jnp.where(inside, mean, taken)
    return vector - taken


def build_kernel(part_1, part_3, rows, piece_1, piece_3):
    build_piece(part_1, rows, piece_1)
    build_piece(part_3, rows, piece_3)


def first_kernel(*refs):
    parts, (rows, own_piece, piece_1, piece_3, piece_2) = refs[:4], refs[4:9]
    message, residual, groups, norm = refs[9:]
    rep, _, _ = place_of()
    build_piece(parts[2], rows, piece_2)
    for turn, part in enumerate(parts):
        source = lax.rem(rep + turn, REPS)
        for block in range(BLKS):
            lines = pl.ds(row_of(source, block * 2), 2)
            residual[lines, :] = part[block, 2, 0:2, :]
            groups[lines, :] = part[block, 2, 2:4, :]
    start = -project(residual[...], groups[...])
    residual[...] = start
    norm[...] = jnp.broadcast_to(total_of(start * start), norm.shape)
    write_message(apply_rows((own_piece, piece_1, piece_2, piece_3), residual, rep), message)


def update(image, residual, direction, charges, groups, norm, residual_out, direction_out, charges_out):
    norm_now = norm[0:1, 0:1]
    along, whole = direction[...], image[...]
    step = norm_now / total_of(along * whole)
    charges_out[...] = step * along if charges is None else charges[...] + step * along
    left = residual[...] - step * project(whole, groups[...])
    residual_out[...] = left
    norm_next = total_of(left * left)
    direction_out[...] = left + norm_next / norm_now * along
    return norm_next


def iterate_kernel(*refs, begun):
    image, residual, direction = refs[:3]
    charges = refs[3] if begun else None
    groups, norm, *pieces = refs[3 + begun : 9 + begun]
    message, residual_out, direction_out, charges_out, norm_out = refs[9 + begun :]
    norm_next = update(image, residual, direction, charges, groups, norm, residual_out, direction_out, charges_out)
    norm_out[...] = jnp.broadcast_to(norm_next, norm_out.shape)
    write_message(apply_rows(pieces, direction_out, place_of()[0]), message)


def last_kernel(
    image, residual, direction, charges, groups, norm, own, piece_1, piece_2, piece_3, share, message, *scratch
):
    residual_out, direction_out, charges_out = scratch
    rep, own_block, window = place_of()
    norm_next = update(image, residual, direction, charges, groups, norm, residual_out, direction_out, charges_out)
    applied = apply_rows((own, piece_1, piece_2, piece_3), direction_out, rep)
    line = row_of(rep, own_block * 2)
    part = applied[0] * direction_out[pl.ds(line, 1), :] + applied[1] * direction_out[pl.ds(line + 1, 1), :]
    share[...] = jnp.broadcast_to(jnp.sum(part, axis=1, keepdims=True) / norm_next, share.shape)
    for core in range(2):
        lines = pl.ds(row_of(rep, core * BLKS) + lax.rem(window // 2, 2), BLKS // 2, stride=2)
        half = slice(core * BLKS // 2, core * BLKS // 2 + BLKS // 2)
        message[half, :] = jnp.where(window < 4, charges_out[lines, :], direction_out[lines, :])


def join_kernel(shares, message, out):
    _, _, window = place_of()
    lane = lax.broadcasted_iota(jnp.int32, message.shape, 1)
    out[...] = jnp.where(lane // WINDOW == lax.rem(window, 2), message[...], total_of(shares[:, 0:1]))


def input_layer_kernel(features, layer_in, layer_bias, out):
    frame = lax.axis_index("phase")
    for kind in range(ELEMS):
        product = jnp.dot(layer_in[:, kind, :], features[frame], precision=highest, preferred_element_type=float32)
        out[kind] = product + as_column(layer_bias[kind : kind + 1, :])


def finish_kernel(parts, inputs, kinds, layer_charge, layer_mid, layer_out, charges_out, energies_out):
    frame = lax.axis_index("phase")
    block = parts[...]
    lane = lax.broadcasted_iota(jnp.int32, block.shape, 1) // WINDOW
    place = lax.broadcasted_iota(jnp.int32, block.shape, 0)
    solved = place // 4 % 4 == lax.rem(frame + 2, 4)
    sender = place // 16 * 4 + place % 4
    inside = lane == sender % 2
    lines = [
        jnp.sum(jnp.where(inside & solved & (sender // 2 == line), block, 0.0), axis=0, keepdims=True)
        for line in range(4)
    ]
    step = LANES - WINDOW
    step = step / total_of(jnp.where(solved & ~inside, block, 0.0))
    charges = jnp.concatenate([lines[0] + step * lines[2], lines[1] + step * lines[3]], axis=1)
    charges_out[...] = charges
    outs = []
    for kind in range(ELEMS):
        hidden_one = jnp.tanh(inputs[kind] + as_column(layer_charge[kind : kind + 1, :]) * charges)
        outs.append(last_layers(layer_mid, layer_out, hidden_one, kind))
    own = pl.ds(pl.multiple_of(lax.axis_index("rep") * OWN, OWN), OWN)
    energies_out[...] = jnp.where(kinds[pl.ds(frame, 1), own] == 1, outs[1], outs[0])


def call(kernel, outs, name, scratch=(), flops=0, held=VMEM):
    def run(*args):
        many = isinstance(outs, list)
        return pl.pallas_call(
            kernel,
            out_shape=outs,
            in_specs=[held] * len(args),
            out_specs=[VMEM] * len(outs) if many else VMEM,
            scratch_shapes=list(scratch),
            compiler_params=PARAMS,
            cost_estimate=pl.CostEstimate(flops=flops, bytes_accessed=0, transcendentals=0) if flops else None,
            name=name,
        )(*args)

    return run


def on_device(
    descriptors,
    positions,
    elements,
    fragments,
    neg_input,
    neg_bias,
    neg_hidden,
    neg_output,
    short_input,
    short_charge,
    short_bias,
    short_hidden,
    short_output,
    widths,
    hardness,
):
    all_axes = ("phase", "zq", "zr", "core", "rep")
    piece = pltpu.VMEM((PIECE, OWN, LANES), float32)
    rows = pltpu.VMEM((5, OWN, LANES), float32)
    whole = shaped(ROWS, LANES)
    small = shaped(8, LANES)

    def exchange(message):
        sent = message.reshape(ROWS // 2, 2, LANES)
        return lax.all_to_all(sent, all_axes, 0, 0, axis_index_groups=cube_groups()).reshape(ROWS, LANES)

    def kept(pieces):
        return [pltpu.with_memory_space_constraint(one, pltpu.VMEM) for one in pieces]

    def turned(layer):
        return jnp.transpose(layer, (1, 0, 2))

    given = [descriptors, turned(positions), elements, fragments, turned(neg_input), neg_bias, turned(neg_hidden)]
    given += [neg_output, widths[None, :], hardness[None, :]]
    held = [pltpu.VMEM(one.shape, one.dtype) for one in given]
    held[1] = pltpu.VMEM((3, elements.shape[0], OWN), float32)
    held[2] = pltpu.VMEM((elements.shape[0], OWN), jnp.int32)
    message, constants = call(
        prepare_kernel,
        [shaped(BLKS, 3, 4, LANES), small],
        "prepare",
        held + [pltpu.SemaphoreType.DMA((len(given),))],
        held=pl.BlockSpec(memory_space=pl.ANY),
    )(*[pltpu.with_memory_space_constraint(one, pltpu.HBM) for one in given])
    atoms_own = lax.all_to_all(message, all_axes, 0, 0, axis_index_groups=block_groups())
    parts = [
        lax.ppermute(atoms_own, "rep", [((rep + turn) % REPS, rep) for rep in range(REPS)]) for turn in range(1, REPS)
    ]
    own_piece, row_values = call(build_own_kernel, [piece, rows], "build_own", flops=10**9)(atoms_own, constants)
    piece_1, piece_3 = call(build_kernel, [piece] * 2, "build_next", flops=2 * 10**9)(
        parts[0], parts[2], *kept([row_values])
    )
    piece_2, message, residual, groups, norm = call(
        first_kernel, [piece, whole, whole, whole, small], "build_rest_and_begin"
    )(atoms_own, *parts, *kept([row_values, own_piece, piece_1, piece_3]))
    pieces = [own_piece, piece_1, piece_2, piece_3]
    message, residual, direction, charges, norm = call(
        functools.partial(iterate_kernel, begun=0), [whole, whole, whole, whole, small], "iterate"
    )(exchange(message), residual, residual, groups, norm, *kept(pieces))
    message, residual, direction, charges, norm = call(
        functools.partial(iterate_kernel, begun=1), [whole, whole, whole, whole, small], "iterate"
    )(exchange(message), residual, direction, charges, groups, norm, *kept(pieces))
    share, message = call(
        last_kernel, [shaped(16, LANES), shaped(BLKS, LANES)], "last", [pltpu.VMEM((ROWS, LANES), float32)] * 3
    )(exchange(message), residual, direction, charges, groups, norm, *kept(pieces))
    shares = lax.all_to_all(share.reshape(16, 1, LANES), all_axes, 0, 0, axis_index_groups=layer_groups())
    shares = shares.reshape(16, LANES)
    message = call(join_kernel, shaped(BLKS, LANES), "join")(shares, message)
    parts = lax.all_to_all(
        message.reshape(BLKS, 1, LANES), all_axes, 0, 0, axis_index_groups=block_groups()
    ).reshape(BLKS, LANES)
    inputs = call(input_layer_kernel, shaped(ELEMS, short_bias.shape[1], OWN), "input_layer", flops=10**7)(
        descriptors, turned(short_input), short_bias
    )
    return call(finish_kernel, [shaped(1, OWN), shaped(1, OWN)], "finish")(
        parts, inputs, elements, short_charge, turned(short_hidden), short_output
    )


def solution(mesh):
    split = Mesh(mesh.devices.reshape(4, 4, 4, 2, 4), ("phase", "zq", "zr", "core", "rep"))
    block_axes = ("zq", "zr", "core")
    return jax.shard_map(
        on_device,
        mesh=split,
        in_specs=(
            P(None, None, block_axes + ("rep",)),
            P(None, None, block_axes),
            P(None, block_axes),
            P(None, block_axes + ("rep",)),
        )
        + (P(),) * 11,
        out_specs=(P("phase", block_axes + ("rep",)), P("phase", block_axes + ("rep",))),
        check_vma=False,
    )
```

```python
import functools

import jax
import jax.numpy as jnp
import numpy as np
from jax import lax
from jax.experimental import pallas as pl
from jax.experimental.pallas import tpu as pltpu
from jax.sharding import Mesh
from jax.sharding import PartitionSpec as P


FRAGS = 4
ELEMS = 2
LANES = 128
OWN = 256
REPS = 4
BLKS = 32
GROUPS = OWN // 8
PIECE = BLKS * 2
ROWS = REPS * PIECE
WINDOW = 64

highest = lax.Precision.HIGHEST
inv_sqrt_pi = 0.5641895835477563
float32 = jnp.float32
VMEM = pl.BlockSpec(memory_space=pltpu.VMEM)
SMEM = pl.BlockSpec(memory_space=pltpu.SMEM)
PARAMS = pltpu.CompilerParams(vmem_limit_bytes=12 * 2**20)


def shaped(*shape):
    return jax.ShapeDtypeStruct(shape, float32)


def eye(size):
    return lax.broadcasted_iota(jnp.int32, (size, size), 0) == lax.broadcasted_iota(jnp.int32, (size, size), 1)


def as_column(row):
    return jnp.sum(jnp.where(eye(row.shape[1]), row, 0.0), axis=1, keepdims=True)


def as_rows(row):
    return jnp.broadcast_to(row, (LANES, LANES)).T


def total_of(values):
    return jnp.sum(jnp.sum(values, axis=0, keepdims=True), axis=1, keepdims=True)


def last_layers(layer_mid, layer_out, hidden_one, kind):
    hidden_two = jnp.dot(layer_mid[:, kind, :], hidden_one, precision=highest, preferred_element_type=float32)
    return jnp.sum(as_column(layer_out[kind : kind + 1, :]) * jnp.tanh(hidden_two), axis=0, keepdims=True)


def network(layer_in, layer_bias, layer_mid, layer_out, features):
    outs = []
    for kind in range(ELEMS):
        hidden_one = jnp.dot(layer_in[:, kind, :], features, precision=highest, preferred_element_type=float32)
        hidden_one = jnp.tanh(hidden_one + as_column(layer_bias[kind : kind + 1, :]))
        outs.append(last_layers(layer_mid, layer_out, hidden_one, kind))
    return outs


def place_of():
    core, spot = lax.axis_index("core"), lax.axis_index("zr")
    turned = jnp.where(lax.axis_index("zq") < 2, 3 - spot, spot)
    return lax.axis_index("rep"), core * 16 + lax.rem(lax.axis_index("phase") + 2, 4) * 4 + turned, core * 4 + spot


def row_of(rep, line):
    return line // 32 * 128 + lax.rem(rep + 2, 4) * 32 + line % 32


def all_devices():
    return np.arange(512).reshape(4, 4, 4, 2, 4)[[2, 3, 0, 1]][..., [2, 3, 0, 1]]


def listed(groups):
    return [[int(device) for device in group] for group in groups]


def cube_groups():
    devices = all_devices()
    devices[:, :2] = devices[:, :2, ::-1].copy()
    return listed(devices.transpose(1, 3, 4, 0, 2).reshape(4, 128))


def block_groups():
    return listed(all_devices()[:, [2, 3, 0, 1]].transpose(0, 4, 3, 1, 2).reshape(16, BLKS))


def layer_groups():
    return listed(all_devices().transpose(1, 2, 3, 0, 4).reshape(BLKS, 16))


def prepare_kernel(*refs):
    given, (message, constants), held, arrived = refs[:10], refs[10:12], refs[12:22], refs[22]
    own = pl.ds(pl.multiple_of(lax.axis_index("rep") * OWN, OWN), OWN)
    copies = []
    for index, (source, target) in enumerate(zip(given, held)):
        source = source.at[:, :, own] if index == 1 else source.at[:, own] if index == 2 else source
        copies.append(pltpu.make_async_copy(source, target, arrived.at[index]))
        copies[-1].start()
    features, coords, kinds, groups, layer_in, layer_bias, layer_mid, layer_out, widths, hardness = held
    frames = features.shape[0]

    def send(frame, pair, one, two):
        block = jnp.concatenate([one[:, :LANES], one[:, LANES:], two[:, :LANES], two[:, LANES:]], axis=0)
        for target in range(BLKS // frames):
            message[target // 4 * 16 + (frame + 2) % 4 * 4 + target % 4, pair] = block

    for copy in copies[1:]:
        copy.wait()
    for frame in range(frames):
        send(frame, 0, coords[0, frame : frame + 1, :], coords[1, frame : frame + 1, :])
        send(frame, 1, coords[2, frame : frame + 1, :], kinds[frame : frame + 1, :].astype(float32))
    for line, source in enumerate((widths, hardness)):
        for kind in range(ELEMS):
            row = jnp.broadcast_to(source[0:1, kind : kind + 1], (1, LANES))
            constants[2 * line + kind : 2 * line + kind + 1, :] = row
    copies[0].wait()
    wide = jnp.concatenate([features[frame] for frame in range(frames)], axis=1)
    first, second = network(layer_in, layer_bias, layer_mid, layer_out, wide)
    for frame in range(frames):
        span = slice(frame * OWN, frame * OWN + OWN)
        electroneg = jnp.where(kinds[frame : frame + 1, :] == 1, second[:, span], first[:, span])
        send(frame, 2, electroneg, groups[frame : frame + 1, :].astype(float32))


def fill_rows(atoms, own_block, constants, rows):
    narrow, broad = constants[0:1, 0:1], constants[1:2, 0:1]
    for half in range(2):
        span = slice(half * LANES, half * LANES + LANES)
        for axis, (pair, line) in enumerate(((0, 0), (0, 2), (1, 0))):
            rows[axis, span] = as_rows(atoms[own_block, pair, line + half : line + half + 1, :])
        kind = as_rows(atoms[own_block, 1, 2 + half : 3 + half, :])
        width = jnp.where(kind > 0.5, broad, narrow)
        rows[3, span] = lax.rsqrt(width * width + narrow * narrow)
        rows[4, span] = lax.rsqrt(width * width + broad * broad)


def build_piece(atoms, rows, piece):
    def one_block(block, carry):
        for half in range(2):
            x, y, z, kind = (
                jnp.broadcast_to(atoms[block, pair, line + half : line + half + 1, :], (8, LANES))
                for pair, line in ((0, 0), (0, 2), (1, 0), (1, 2))
            )
            second = kind > 0.5
            for group in range(GROUPS):
                span = slice(group * 8, group * 8 + 8)
                delta_x = rows[0, span] - x
                delta_y = rows[1, span] - y
                delta_z = rows[2, span] - z
                squared = delta_x * delta_x + delta_y * delta_y + delta_z * delta_z
                inverse = lax.rsqrt(squared)
                scale = jnp.where(second, rows[4, span], rows[3, span])
                piece[2 * block + half, span, :] = lax.erf(squared * inverse * scale) * inverse
        return carry

    lax.fori_loop(0, BLKS, one_block, 0, unroll=2)


def build_own_kernel(atoms, constants, piece, rows):
    _, own_block, _ = place_of()
    fill_rows(atoms, own_block, constants, rows)
    build_piece(atoms, rows, piece)
    width_0, width_1, hardness_0, hardness_1 = (constants[line : line + 1, 0:1] for line in range(4))
    for half in range(2):
        span = slice(half * LANES, half * LANES + LANES)
        second = as_rows(atoms[own_block, 1, 2 + half : 3 + half, :]) > 0.5
        diagonal = jnp.where(second, hardness_1, hardness_0) + inv_sqrt_pi / jnp.where(second, width_1, width_0)
        tile = piece[2 * own_block + half, span, :]
        piece[2 * own_block + half, span, :] = jnp.where(eye(LANES), diagonal, tile)


def apply_rows(pieces, direction, rep):
    sums = tuple(jnp.zeros((8, LANES), float32) for _ in range(GROUPS))
    for turn, piece in enumerate(pieces):
        for core in range(2):
            first = row_of(lax.rem(rep + turn, REPS), core * BLKS)

            def one_line(line, sums, core=core, piece=piece, first=first):
                values = jnp.broadcast_to(direction[pl.ds(first + line, 1), :], (8, LANES))
                here = core * BLKS + line
                return tuple(
                    sums[group] + piece[here, group * 8 : group * 8 + 8, :] * values for group in range(GROUPS)
                )

            sums = lax.fori_loop(0, BLKS, one_line, sums, unroll=8)
    half = GROUPS // 2
    return [
        jnp.sum(jnp.concatenate(sums[part * half : part * half + half], axis=0).T, axis=0, keepdims=True)
        for part in range(2)
    ]


def write_message(image, message):
    block = jnp.concatenate(image * 4, axis=0)
    for line in range(ROWS // 8):
        message[line * 8 : line * 8 + 8, :] = block


def project(vector, groups):
    members = ROWS * LANES // FRAGS
    taken = jnp.zeros_like(vector)
    for group in range(FRAGS):
        inside = groups == float(group)
        mean = total_of(jnp.where(inside, vector, 0.0)) / members
        taken = jnp.where(inside, mean, taken)
    return vector - taken


def build_kernel(part_1, rows, piece_1):
    build_piece(part_1, rows, piece_1)


def first_kernel(*refs):
    parts, (rows, own_piece, piece_1, piece_3, piece_2) = refs[:4], refs[4:9]
    message, residual, groups, norm = refs[9:]
    rep, _, _ = place_of()
    build_piece(parts[3], rows, piece_3)
    build_piece(parts[2], rows, piece_2)
    for turn, part in enumerate(parts):
        source = lax.rem(rep + turn, REPS)
        for block in range(BLKS):
            lines = pl.ds(row_of(source, block * 2), 2)
            residual[lines, :] = part[block, 2, 0:2, :]
            groups[lines, :] = part[block, 2, 2:4, :]
    start = -project(residual[...], groups[...])
    residual[...] = start
    norm[...] = jnp.broadcast_to(total_of(start * start), norm.shape)
    write_message(apply_rows((own_piece, piece_1, piece_2, piece_3), residual, rep), message)


def update(image, residual, direction, charges, groups, norm, residual_out, direction_out, charges_out):
    norm_now = norm[0:1, 0:1]
    along, whole = direction[...], image[...]
    step = norm_now / total_of(along * whole)
    charges_out[...] = step * along if charges is None else charges[...] + step * along
    left = residual[...] - step * project(whole, groups[...])
    residual_out[...] = left
    norm_next = total_of(left * left)
    direction_out[...] = left + norm_next / norm_now * along
    return norm_next


def iterate_kernel(*refs, begun):
    image, residual, direction = refs[:3]
    charges = refs[3] if begun else None
    groups, norm, *pieces = refs[3 + begun : 9 + begun]
    message, residual_out, direction_out, charges_out, norm_out = refs[9 + begun :]
    norm_next = update(image, residual, direction, charges, groups, norm, residual_out, direction_out, charges_out)
    norm_out[...] = jnp.broadcast_to(norm_next, norm_out.shape)
    write_message(apply_rows(pieces, direction_out, place_of()[0]), message)


def last_kernel(
    image, residual, direction, charges, groups, norm, own, piece_1, piece_2, piece_3, share, message, *scratch
):
    residual_out, direction_out, charges_out = scratch
    rep, own_block, window = place_of()
    norm_next = update(image, residual, direction, charges, groups, norm, residual_out, direction_out, charges_out)
    applied = apply_rows((own, piece_1, piece_2, piece_3), direction_out, rep)
    line = row_of(rep, own_block * 2)
    part = applied[0] * direction_out[pl.ds(line, 1), :] + applied[1] * direction_out[pl.ds(line + 1, 1), :]
    share[...] = jnp.broadcast_to(jnp.sum(part, axis=1, keepdims=True) / norm_next, share.shape)
    for core in range(2):
        lines = pl.ds(row_of(rep, core * BLKS) + lax.rem(window // 2, 2), BLKS // 2, stride=2)
        half = slice(core * BLKS // 2, core * BLKS // 2 + BLKS // 2)
        message[half, :] = jnp.where(window < 4, charges_out[lines, :], direction_out[lines, :])


def join_kernel(shares, message, out):
    _, _, window = place_of()
    lane = lax.broadcasted_iota(jnp.int32, message.shape, 1)
    out[...] = jnp.where(lane // WINDOW == lax.rem(window, 2), message[...], total_of(shares[:, 0:1]))


def input_layer_kernel(features, layer_in, layer_bias, out):
    frame = lax.axis_index("phase")
    for kind in range(ELEMS):
        product = jnp.dot(layer_in[:, kind, :], features[frame], precision=highest, preferred_element_type=float32)
        out[kind] = product + as_column(layer_bias[kind : kind + 1, :])


def finish_kernel(parts, inputs, kinds, layer_charge, layer_mid, layer_out, charges_out, energies_out):
    frame = lax.axis_index("phase")
    block = parts[...]
    lane = lax.broadcasted_iota(jnp.int32, block.shape, 1) // WINDOW
    place = lax.broadcasted_iota(jnp.int32, block.shape, 0)
    solved = place // 4 % 4 == lax.rem(frame + 2, 4)
    sender = place // 16 * 4 + place % 4
    inside = lane == sender % 2
    lines = [
        jnp.sum(jnp.where(inside & solved & (sender // 2 == line), block, 0.0), axis=0, keepdims=True)
        for line in range(4)
    ]
    step = LANES - WINDOW
    step = step / total_of(jnp.where(solved & ~inside, block, 0.0))
    charges = jnp.concatenate([lines[0] + step * lines[2], lines[1] + step * lines[3]], axis=1)
    charges_out[...] = charges
    outs = []
    for kind in range(ELEMS):
        hidden_one = jnp.tanh(inputs[kind] + as_column(layer_charge[kind : kind + 1, :]) * charges)
        outs.append(last_layers(layer_mid, layer_out, hidden_one, kind))
    own = pl.ds(pl.multiple_of(lax.axis_index("rep") * OWN, OWN), OWN)
    energies_out[...] = jnp.where(kinds[pl.ds(frame, 1), own] == 1, outs[1], outs[0])


def call(kernel, outs, name, scratch=(), flops=0, held=VMEM):
    def run(*args):
        many = isinstance(outs, list)
        return pl.pallas_call(
            kernel,
            out_shape=outs,
            in_specs=[held] * len(args),
            out_specs=[VMEM] * len(outs) if many else VMEM,
            scratch_shapes=list(scratch),
            compiler_params=PARAMS,
            cost_estimate=pl.CostEstimate(flops=flops, bytes_accessed=0, transcendentals=0) if flops else None,
            name=name,
        )(*args)

    return run


def on_device(
    descriptors,
    positions,
    elements,
    fragments,
    neg_input,
    neg_bias,
    neg_hidden,
    neg_output,
    short_input,
    short_charge,
    short_bias,
    short_hidden,
    short_output,
    widths,
    hardness,
):
    all_axes = ("phase", "zq", "zr", "core", "rep")
    piece = pltpu.VMEM((PIECE, OWN, LANES), float32)
    rows = pltpu.VMEM((5, OWN, LANES), float32)
    whole = shaped(ROWS, LANES)
    small = shaped(8, LANES)

    def exchange(message):
        sent = message.reshape(ROWS // 2, 2, LANES)
        return lax.all_to_all(sent, all_axes, 0, 0, axis_index_groups=cube_groups()).reshape(ROWS, LANES)

    def kept(pieces):
        return [pltpu.with_memory_space_constraint(one, pltpu.VMEM) for one in pieces]

    def turned(layer):
        return jnp.transpose(layer, (1, 0, 2))

    given = [descriptors, turned(positions), elements, fragments, turned(neg_input), neg_bias, turned(neg_hidden)]
    given += [neg_output, widths[None, :], hardness[None, :]]
    held = [pltpu.VMEM(one.shape, one.dtype) for one in given]
    held[1] = pltpu.VMEM((3, elements.shape[0], OWN), float32)
    held[2] = pltpu.VMEM((elements.shape[0], OWN), jnp.int32)
    message, constants = call(
        prepare_kernel,
        [shaped(BLKS, 3, 4, LANES), small],
        "prepare",
        held + [pltpu.SemaphoreType.DMA((len(given),))],
        held=pl.BlockSpec(memory_space=pl.ANY),
    )(*[pltpu.with_memory_space_constraint(one, pltpu.HBM) for one in given])
    atoms_own = lax.all_to_all(message, all_axes, 0, 0, axis_index_groups=block_groups())
    parts = [
        lax.ppermute(atoms_own, "rep", [((rep + turn) % REPS, rep) for rep in range(REPS)]) for turn in range(1, REPS)
    ]
    own_piece, row_values = call(build_own_kernel, [piece, rows], "build_own", flops=10**9)(atoms_own, constants)
    piece_1 = call(build_kernel, piece, "build_next", flops=10**9)(parts[0], *kept([row_values]))
    piece_3, piece_2, message, residual, groups, norm = call(
        first_kernel, [piece, piece, whole, whole, whole, small], "build_rest_and_begin"
    )(atoms_own, *parts, *kept([row_values, own_piece, piece_1]))
    pieces = [own_piece, piece_1, piece_2, piece_3]
    message, residual, direction, charges, norm = call(
        functools.partial(iterate_kernel, begun=0), [whole, whole, whole, whole, small], "iterate"
    )(exchange(message), residual, residual, groups, norm, *kept(pieces))
    message, residual, direction, charges, norm = call(
        functools.partial(iterate_kernel, begun=1), [whole, whole, whole, whole, small], "iterate"
    )(exchange(message), residual, direction, charges, groups, norm, *kept(pieces))
    share, message = call(
        last_kernel, [shaped(16, LANES), shaped(BLKS, LANES)], "last", [pltpu.VMEM((ROWS, LANES), float32)] * 3
    )(exchange(message), residual, direction, charges, groups, norm, *kept(pieces))
    shares = lax.all_to_all(share.reshape(16, 1, LANES), all_axes, 0, 0, axis_index_groups=layer_groups())
    shares = shares.reshape(16, LANES)
    message = call(join_kernel, shaped(BLKS, LANES), "join")(shares, message)
    parts = lax.all_to_all(
        message.reshape(BLKS, 1, LANES), all_axes, 0, 0, axis_index_groups=block_groups()
    ).reshape(BLKS, LANES)
    inputs = call(input_layer_kernel, shaped(ELEMS, short_bias.shape[1], OWN), "input_layer", flops=10**7)(
        descriptors, turned(short_input), short_bias
    )
    return call(finish_kernel, [shaped(1, OWN), shaped(1, OWN)], "finish")(
        parts, inputs, elements, short_charge, turned(short_hidden), short_output
    )


def solution(mesh):
    split = Mesh(mesh.devices.reshape(4, 4, 4, 2, 4), ("phase", "zq", "zr", "core", "rep"))
    block_axes = ("zq", "zr", "core")
    return jax.shard_map(
        on_device,
        mesh=split,
        in_specs=(
            P(None, None, block_axes + ("rep",)),
            P(None, None, block_axes),
            P(None, block_axes),
            P(None, block_axes + ("rep",)),
        )
        + (P(),) * 11,
        out_specs=(P("phase", block_axes + ("rep",)), P("phase", block_axes + ("rep",))),
        check_vma=False,
    )
```

```python
import functools

import jax
import jax.numpy as jnp
import numpy as np
from jax import lax
from jax.experimental import pallas as pl
from jax.experimental.pallas import tpu as pltpu
from jax.sharding import Mesh
from jax.sharding import PartitionSpec as P


FRAGS = 4
ELEMS = 2
LANES = 128
OWN = 256
REPS = 4
BLKS = 32
GROUPS = OWN // 8
PIECE = BLKS * 2
ROWS = REPS * PIECE
WINDOW = 64

highest = lax.Precision.HIGHEST
inv_sqrt_pi = 0.5641895835477563
float32 = jnp.float32
VMEM = pl.BlockSpec(memory_space=pltpu.VMEM)
SMEM = pl.BlockSpec(memory_space=pltpu.SMEM)
PARAMS = pltpu.CompilerParams(vmem_limit_bytes=12 * 2**20)


def shaped(*shape):
    return jax.ShapeDtypeStruct(shape, float32)


def eye(size):
    return lax.broadcasted_iota(jnp.int32, (size, size), 0) == lax.broadcasted_iota(jnp.int32, (size, size), 1)


def as_column(row):
    return jnp.sum(jnp.where(eye(row.shape[1]), row, 0.0), axis=1, keepdims=True)


def as_rows(row):
    return jnp.broadcast_to(row, (LANES, LANES)).T


def total_of(values):
    return jnp.sum(jnp.sum(values, axis=0, keepdims=True), axis=1, keepdims=True)


def last_layers(layer_mid, layer_out, hidden_one, kind):
    hidden_two = jnp.dot(layer_mid[:, kind, :], hidden_one, precision=highest, preferred_element_type=float32)
    return jnp.sum(as_column(layer_out[kind : kind + 1, :]) * jnp.tanh(hidden_two), axis=0, keepdims=True)


def network(layer_in, layer_bias, layer_mid, layer_out, features):
    outs = []
    for kind in range(ELEMS):
        hidden_one = jnp.dot(layer_in[:, kind, :], features, precision=highest, preferred_element_type=float32)
        hidden_one = jnp.tanh(hidden_one + as_column(layer_bias[kind : kind + 1, :]))
        outs.append(last_layers(layer_mid, layer_out, hidden_one, kind))
    return outs


def place_of():
    core, spot = lax.axis_index("core"), lax.axis_index("zr")
    turned = jnp.where(lax.axis_index("zq") < 2, 3 - spot, spot)
    return lax.axis_index("rep"), core * 16 + lax.rem(lax.axis_index("phase") + 2, 4) * 4 + turned, core * 4 + spot


def row_of(rep, line):
    return line // 32 * 128 + lax.rem(rep + 2, 4) * 32 + line % 32


def all_devices():
    return np.arange(512).reshape(4, 4, 4, 2, 4)[[2, 3, 0, 1]][..., [2, 3, 0, 1]]


def listed(groups):
    return [[int(device) for device in group] for group in groups]


def cube_groups():
    devices = all_devices()
    devices[:, :2] = devices[:, :2, ::-1].copy()
    return listed(devices.transpose(1, 3, 4, 0, 2).reshape(4, 128))


def block_groups():
    return listed(all_devices()[:, [2, 3, 0, 1]].transpose(0, 4, 3, 1, 2).reshape(16, BLKS))


def layer_groups():
    return listed(all_devices().transpose(1, 2, 3, 0, 4).reshape(BLKS, 16))


def prepare_kernel(*refs):
    given, (message, constants), held, arrived = refs[:10], refs[10:12], refs[12:22], refs[22]
    own = pl.ds(pl.multiple_of(lax.axis_index("rep") * OWN, OWN), OWN)
    copies = []
    for index, (source, target) in enumerate(zip(given, held)):
        source = source.at[:, :, own] if index == 1 else source.at[:, own] if index == 2 else source
        copies.append(pltpu.make_async_copy(source, target, arrived.at[index]))
        copies[-1].start()
    features, coords, kinds, groups, layer_in, layer_bias, layer_mid, layer_out, widths, hardness = held
    frames = features.shape[0]

    def send(frame, pair, one, two):
        block = jnp.concatenate([one[:, :LANES], one[:, LANES:], two[:, :LANES], two[:, LANES:]], axis=0)
        for target in range(BLKS // frames):
            message[target // 4 * 16 + (frame + 2) % 4 * 4 + target % 4, pair] = block

    for copy in copies[1:]:
        copy.wait()
    for frame in range(frames):
        send(frame, 0, coords[0, frame : frame + 1, :], coords[1, frame : frame + 1, :])
        send(frame, 1, coords[2, frame : frame + 1, :], kinds[frame : frame + 1, :].astype(float32))
    for line, source in enumerate((widths, hardness)):
        for kind in range(ELEMS):
            row = jnp.broadcast_to(source[0:1, kind : kind + 1], (1, LANES))
            constants[2 * line + kind : 2 * line + kind + 1, :] = row
    copies[0].wait()
    wide = jnp.concatenate([features[frame] for frame in range(frames)], axis=1)
    first, second = network(layer_in, layer_bias, layer_mid, layer_out, wide)
    for frame in range(frames):
        span = slice(frame * OWN, frame * OWN + OWN)
        electroneg = jnp.where(kinds[frame : frame + 1, :] == 1, second[:, span], first[:, span])
        send(frame, 2, electroneg, groups[frame : frame + 1, :].astype(float32))


def fill_rows(atoms, own_block, constants, rows):
    narrow, broad = constants[0:1, 0:1], constants[1:2, 0:1]
    for half in range(2):
        span = slice(half * LANES, half * LANES + LANES)
        for axis, (pair, line) in enumerate(((0, 0), (0, 2), (1, 0))):
            rows[axis, span] = as_rows(atoms[own_block, pair, line + half : line + half + 1, :])
        kind = as_rows(atoms[own_block, 1, 2 + half : 3 + half, :])
        width = jnp.where(kind > 0.5, broad, narrow)
        rows[3, span] = lax.rsqrt(width * width + narrow * narrow)
        rows[4, span] = lax.rsqrt(width * width + broad * broad)


def build_piece(atoms, rows, piece):
    def one_block(block, carry):
        for half in range(2):
            x, y, z, kind = (
                jnp.broadcast_to(atoms[block, pair, line + half : line + half + 1, :], (8, LANES))
                for pair, line in ((0, 0), (0, 2), (1, 0), (1, 2))
            )
            second = kind > 0.5
            for group in range(GROUPS):
                span = slice(group * 8, group * 8 + 8)
                delta_x = rows[0, span] - x
                delta_y = rows[1, span] - y
                delta_z = rows[2, span] - z
                squared = delta_x * delta_x + delta_y * delta_y + delta_z * delta_z
                inverse = lax.rsqrt(squared)
                scale = jnp.where(second, rows[4, span], rows[3, span])
                piece[2 * block + half, span, :] = lax.erf(squared * inverse * scale) * inverse
        return carry

    lax.fori_loop(0, BLKS, one_block, 0, unroll=4)


def build_own_kernel(atoms, constants, piece, rows):
    _, own_block, _ = place_of()
    fill_rows(atoms, own_block, constants, rows)
    build_piece(atoms, rows, piece)
    width_0, width_1, hardness_0, hardness_1 = (constants[line : line + 1, 0:1] for line in range(4))
    for half in range(2):
        span = slice(half * LANES, half * LANES + LANES)
        second = as_rows(atoms[own_block, 1, 2 + half : 3 + half, :]) > 0.5
        diagonal = jnp.where(second, hardness_1, hardness_0) + inv_sqrt_pi / jnp.where(second, width_1, width_0)
        tile = piece[2 * own_block + half, span, :]
        piece[2 * own_block + half, span, :] = jnp.where(eye(LANES), diagonal, tile)


def apply_rows(pieces, direction, rep):
    sums = tuple(jnp.zeros((8, LANES), float32) for _ in range(GROUPS))
    for turn, piece in enumerate(pieces):
        for core in range(2):
            first = row_of(rep ^ turn, core * BLKS)

            def one_line(line, sums, core=core, piece=piece, first=first):
                values = jnp.broadcast_to(direction[pl.ds(first + line, 1), :], (8, LANES))
                here = core * BLKS + line
                return tuple(
                    sums[group] + piece[here, group * 8 : group * 8 + 8, :] * values for group in range(GROUPS)
                )

            sums = lax.fori_loop(0, BLKS, one_line, sums, unroll=8)
    half = GROUPS // 2
    return [
        jnp.sum(jnp.concatenate(sums[part * half : part * half + half], axis=0).T, axis=0, keepdims=True)
        for part in range(2)
    ]


def write_message(image, message):
    block = jnp.concatenate(image * 4, axis=0)
    for line in range(ROWS // 8):
        message[line * 8 : line * 8 + 8, :] = block


def project(vector, groups):
    members = ROWS * LANES // FRAGS
    taken = jnp.zeros_like(vector)
    for group in range(FRAGS):
        inside = groups == float(group)
        mean = total_of(jnp.where(inside, vector, 0.0)) / members
        taken = jnp.where(inside, mean, taken)
    return vector - taken


def build_kernel(part_1, rows, piece_1):
    build_piece(part_1, rows, piece_1)


def first_kernel(*refs):
    parts, (rows, own_piece, piece_1, piece_3, piece_2) = refs[:4], refs[4:9]
    message, residual, groups, norm = refs[9:]
    rep, _, _ = place_of()
    build_piece(parts[3], rows, piece_3)
    build_piece(parts[2], rows, piece_2)
    for turn, part in enumerate(parts):
        source = rep ^ turn
        for block in range(BLKS):
            lines = pl.ds(row_of(source, block * 2), 2)
            residual[lines, :] = part[block, 2, 0:2, :]
            groups[lines, :] = part[block, 2, 2:4, :]
    start = -project(residual[...], groups[...])
    residual[...] = start
    norm[...] = jnp.broadcast_to(total_of(start * start), norm.shape)
    write_message(apply_rows((own_piece, piece_1, piece_2, piece_3), residual, rep), message)


def update(image, residual, direction, charges, groups, norm, residual_out, direction_out, charges_out):
    norm_now = norm[0:1, 0:1]
    along, whole = direction[...], image[...]
    step = norm_now / total_of(along * whole)
    charges_out[...] = step * along if charges is None else charges[...] + step * along
    left = residual[...] - step * project(whole, groups[...])
    residual_out[...] = left
    norm_next = total_of(left * left)
    direction_out[...] = left + norm_next / norm_now * along
    return norm_next


def iterate_kernel(*refs, begun):
    image, residual, direction = refs[:3]
    charges = refs[3] if begun else None
    groups, norm, *pieces = refs[3 + begun : 9 + begun]
    message, residual_out, direction_out, charges_out, norm_out = refs[9 + begun :]
    norm_next = update(image, residual, direction, charges, groups, norm, residual_out, direction_out, charges_out)
    norm_out[...] = jnp.broadcast_to(norm_next, norm_out.shape)
    write_message(apply_rows(pieces, direction_out, place_of()[0]), message)


def last_kernel(
    image, residual, direction, charges, groups, norm, own, piece_1, piece_2, piece_3, share, message, *scratch
):
    residual_out, direction_out, charges_out = scratch
    rep, own_block, window = place_of()
    norm_next = update(image, residual, direction, charges, groups, norm, residual_out, direction_out, charges_out)
    applied = apply_rows((own, piece_1, piece_2, piece_3), direction_out, rep)
    line = row_of(rep, own_block * 2)
    part = applied[0] * direction_out[pl.ds(line, 1), :] + applied[1] * direction_out[pl.ds(line + 1, 1), :]
    share[...] = jnp.broadcast_to(jnp.sum(part, axis=1, keepdims=True) / norm_next, share.shape)
    for core in range(2):
        lines = pl.ds(row_of(rep, core * BLKS) + lax.rem(window // 2, 2), BLKS // 2, stride=2)
        half = slice(core * BLKS // 2, core * BLKS // 2 + BLKS // 2)
        message[half, :] = jnp.where(window < 4, charges_out[lines, :], direction_out[lines, :])


def join_kernel(shares, message, out):
    _, _, window = place_of()
    lane = lax.broadcasted_iota(jnp.int32, message.shape, 1)
    out[...] = jnp.where(lane // WINDOW == lax.rem(window, 2), message[...], total_of(shares[:, 0:1]))


def finish_kernel(
    parts, features, kinds, layer_in, layer_charge, layer_bias, layer_mid, layer_out, charges_out, energies_out
):
    frame = lax.axis_index("phase")
    inputs = [
        jnp.dot(layer_in[:, kind, :], features[frame], precision=highest, preferred_element_type=float32)
        + as_column(layer_bias[kind : kind + 1, :])
        for kind in range(ELEMS)
    ]
    block = parts[...]
    lane = lax.broadcasted_iota(jnp.int32, block.shape, 1) // WINDOW
    place = lax.broadcasted_iota(jnp.int32, block.shape, 0)
    solved = place // 4 % 4 == lax.rem(frame + 2, 4)
    sender = place // 16 * 4 + place % 4
    inside = lane == sender % 2
    lines = [
        jnp.sum(jnp.where(inside & solved & (sender // 2 == line), block, 0.0), axis=0, keepdims=True)
        for line in range(4)
    ]
    step = LANES - WINDOW
    step = step / total_of(jnp.where(solved & ~inside, block, 0.0))
    charges = jnp.concatenate([lines[0] + step * lines[2], lines[1] + step * lines[3]], axis=1)
    charges_out[...] = charges
    outs = []
    for kind in range(ELEMS):
        hidden_one = jnp.tanh(inputs[kind] + as_column(layer_charge[kind : kind + 1, :]) * charges)
        outs.append(last_layers(layer_mid, layer_out, hidden_one, kind))
    own = pl.ds(pl.multiple_of(lax.axis_index("rep") * OWN, OWN), OWN)
    energies_out[...] = jnp.where(kinds[pl.ds(frame, 1), own] == 1, outs[1], outs[0])


def call(kernel, outs, name, scratch=(), flops=0, held=VMEM):
    def run(*args):
        many = isinstance(outs, list)
        return pl.pallas_call(
            kernel,
            out_shape=outs,
            in_specs=[held] * len(args),
            out_specs=[VMEM] * len(outs) if many else VMEM,
            scratch_shapes=list(scratch),
            compiler_params=PARAMS,
            cost_estimate=pl.CostEstimate(flops=flops, bytes_accessed=0, transcendentals=0) if flops else None,
            name=name,
        )(*args)

    return run


def on_device(
    descriptors,
    positions,
    elements,
    fragments,
    neg_input,
    neg_bias,
    neg_hidden,
    neg_output,
    short_input,
    short_charge,
    short_bias,
    short_hidden,
    short_output,
    widths,
    hardness,
):
    all_axes = ("phase", "zq", "zr", "core", "rep")
    piece = pltpu.VMEM((PIECE, OWN, LANES), float32)
    rows = pltpu.VMEM((5, OWN, LANES), float32)
    whole = shaped(ROWS, LANES)
    small = shaped(8, LANES)

    def exchange(message):
        sent = message.reshape(ROWS // 2, 2, LANES)
        return lax.all_to_all(sent, all_axes, 0, 0, axis_index_groups=cube_groups()).reshape(ROWS, LANES)

    def kept(pieces):
        return [pltpu.with_memory_space_constraint(one, pltpu.VMEM) for one in pieces]

    def turned(layer):
        return jnp.transpose(layer, (1, 0, 2))

    given = [descriptors, turned(positions), elements, fragments, turned(neg_input), neg_bias, turned(neg_hidden)]
    given += [neg_output, widths[None, :], hardness[None, :]]
    held = [pltpu.VMEM(one.shape, one.dtype) for one in given]
    held[1] = pltpu.VMEM((3, elements.shape[0], OWN), float32)
    held[2] = pltpu.VMEM((elements.shape[0], OWN), jnp.int32)
    message, constants = call(
        prepare_kernel,
        [shaped(BLKS, 3, 4, LANES), small],
        "prepare",
        held + [pltpu.SemaphoreType.DMA((len(given),))],
        held=pl.BlockSpec(memory_space=pl.ANY),
    )(*[pltpu.with_memory_space_constraint(one, pltpu.HBM) for one in given])
    atoms_own = lax.all_to_all(message, all_axes, 0, 0, axis_index_groups=block_groups())
    parts = [
        lax.ppermute(atoms_own, "rep", [(rep ^ turn, rep) for rep in range(REPS)]) for turn in range(1, REPS)
    ]
    own_piece, row_values = call(build_own_kernel, [piece, rows], "build_own", flops=10**9)(atoms_own, constants)
    piece_1 = call(build_kernel, piece, "build_next", flops=10**9)(parts[0], *kept([row_values]))
    piece_3, piece_2, message, residual, groups, norm = call(
        first_kernel, [piece, piece, whole, whole, whole, small], "build_rest_and_begin"
    )(atoms_own, *parts, *kept([row_values, own_piece, piece_1]))
    pieces = [own_piece, piece_1, piece_2, piece_3]
    message, residual, direction, charges, norm = call(
        functools.partial(iterate_kernel, begun=0), [whole, whole, whole, whole, small], "iterate"
    )(exchange(message), residual, residual, groups, norm, *kept(pieces))
    message, residual, direction, charges, norm = call(
        functools.partial(iterate_kernel, begun=1), [whole, whole, whole, whole, small], "iterate"
    )(exchange(message), residual, direction, charges, groups, norm, *kept(pieces))
    share, message = call(
        last_kernel, [shaped(16, LANES), shaped(BLKS, LANES)], "last", [pltpu.VMEM((ROWS, LANES), float32)] * 3
    )(exchange(message), residual, direction, charges, groups, norm, *kept(pieces))
    shares = lax.all_to_all(share.reshape(16, 1, LANES), all_axes, 0, 0, axis_index_groups=layer_groups())
    shares = shares.reshape(16, LANES)
    message = call(join_kernel, shaped(BLKS, LANES), "join")(shares, message)
    parts = lax.all_to_all(
        message.reshape(BLKS, 1, LANES), all_axes, 0, 0, axis_index_groups=block_groups()
    ).reshape(BLKS, LANES)
    return call(finish_kernel, [shaped(1, OWN), shaped(1, OWN)], "finish")(
        parts,
        descriptors,
        elements,
        turned(short_input),
        short_charge,
        short_bias,
        turned(short_hidden),
        short_output,
    )


def solution(mesh):
    split = Mesh(mesh.devices.reshape(4, 4, 4, 2, 4), ("phase", "zq", "zr", "core", "rep"))
    block_axes = ("zq", "zr", "core")
    return jax.shard_map(
        on_device,
        mesh=split,
        in_specs=(
            P(None, None, block_axes + ("rep",)),
            P(None, None, block_axes),
            P(None, block_axes),
            P(None, block_axes + ("rep",)),
        )
        + (P(),) * 11,
        out_specs=(P("phase", block_axes + ("rep",)), P("phase", block_axes + ("rep",))),
        check_vma=False,
    )
```

```python
import functools

import jax
import jax.numpy as jnp
import numpy as np
from jax import lax
from jax.experimental import pallas as pl
from jax.experimental.pallas import tpu as pltpu
from jax.sharding import Mesh
from jax.sharding import PartitionSpec as P


FRAGS = 4
ELEMS = 2
LANES = 128
OWN = 256
REPS = 4
BLKS = 32
GROUPS = OWN // 8
PIECE = BLKS * 2
ROWS = REPS * PIECE
WINDOW = 64

highest = lax.Precision.HIGHEST
inv_sqrt_pi = 0.5641895835477563
float32 = jnp.float32
VMEM = pl.BlockSpec(memory_space=pltpu.VMEM)
SMEM = pl.BlockSpec(memory_space=pltpu.SMEM)
PARAMS = pltpu.CompilerParams(vmem_limit_bytes=12 * 2**20)


def shaped(*shape):
    return jax.ShapeDtypeStruct(shape, float32)


def eye(size):
    return lax.broadcasted_iota(jnp.int32, (size, size), 0) == lax.broadcasted_iota(jnp.int32, (size, size), 1)


def as_column(row):
    return jnp.sum(jnp.where(eye(row.shape[1]), row, 0.0), axis=1, keepdims=True)


def as_rows(row):
    return jnp.broadcast_to(row, (LANES, LANES)).T


def total_of(values):
    return jnp.sum(jnp.sum(values, axis=0, keepdims=True), axis=1, keepdims=True)


def last_layers(layer_mid, layer_out, hidden_one, kind):
    hidden_two = jnp.dot(layer_mid[:, kind, :], hidden_one, precision=highest, preferred_element_type=float32)
    return jnp.sum(as_column(layer_out[kind : kind + 1, :]) * jnp.tanh(hidden_two), axis=0, keepdims=True)


def network(layer_in, layer_bias, layer_mid, layer_out, features):
    outs = []
    for kind in range(ELEMS):
        hidden_one = jnp.dot(layer_in[:, kind, :], features, precision=highest, preferred_element_type=float32)
        hidden_one = jnp.tanh(hidden_one + as_column(layer_bias[kind : kind + 1, :]))
        outs.append(last_layers(layer_mid, layer_out, hidden_one, kind))
    return outs


def place_of():
    core, spot = lax.axis_index("core"), lax.axis_index("zr")
    turned = jnp.where(lax.axis_index("zq") < 2, 3 - spot, spot)
    return lax.axis_index("rep"), core * 16 + lax.rem(lax.axis_index("phase") + 2, 4) * 4 + turned, core * 4 + spot


def row_of(rep, line):
    return line // 32 * 128 + lax.rem(rep + 2, 4) * 32 + line % 32


def all_devices():
    return np.arange(512).reshape(4, 4, 4, 2, 4)[[2, 3, 0, 1]][..., [2, 3, 0, 1]]


def listed(groups):
    return [[int(device) for device in group] for group in groups]


def cube_groups():
    devices = all_devices()
    devices[:, :2] = devices[:, :2, ::-1].copy()
    return listed(devices.transpose(1, 3, 4, 0, 2).reshape(4, 128))


def block_groups():
    return listed(all_devices()[:, [2, 3, 0, 1]].transpose(0, 4, 3, 1, 2).reshape(16, BLKS))


def layer_groups():
    return listed(all_devices().transpose(1, 2, 3, 0, 4).reshape(BLKS, 16))


def prepare_kernel(*refs):
    given, (message, constants), held, arrived = refs[:10], refs[10:12], refs[12:22], refs[22]
    own = pl.ds(pl.multiple_of(lax.axis_index("rep") * OWN, OWN), OWN)
    copies = []
    for index, (source, target) in enumerate(zip(given, held)):
        source = source.at[:, :, own] if index == 1 else source.at[:, own] if index == 2 else source
        copies.append(pltpu.make_async_copy(source, target, arrived.at[index]))
        copies[-1].start()
    features, coords, kinds, groups, layer_in, layer_bias, layer_mid, layer_out, widths, hardness = held
    frames = features.shape[0]

    def send(frame, pair, one, two):
        block = jnp.concatenate([one[:, :LANES], one[:, LANES:], two[:, :LANES], two[:, LANES:]], axis=0)
        for target in range(BLKS // frames):
            message[target // 4 * 16 + (frame + 2) % 4 * 4 + target % 4, pair] = block

    for copy in copies[1:]:
        copy.wait()
    for frame in range(frames):
        send(frame, 0, coords[0, frame : frame + 1, :], coords[1, frame : frame + 1, :])
        send(frame, 1, coords[2, frame : frame + 1, :], kinds[frame : frame + 1, :].astype(float32))
    for line, source in enumerate((widths, hardness)):
        for kind in range(ELEMS):
            row = jnp.broadcast_to(source[0:1, kind : kind + 1], (1, LANES))
            constants[2 * line + kind : 2 * line + kind + 1, :] = row
    copies[0].wait()
    wide = jnp.concatenate([features[frame] for frame in range(frames)], axis=1)
    first, second = network(layer_in, layer_bias, layer_mid, layer_out, wide)
    for frame in range(frames):
        span = slice(frame * OWN, frame * OWN + OWN)
        electroneg = jnp.where(kinds[frame : frame + 1, :] == 1, second[:, span], first[:, span])
        send(frame, 2, electroneg, groups[frame : frame + 1, :].astype(float32))


def fill_rows(atoms, own_block, constants, rows):
    narrow, broad = constants[0:1, 0:1], constants[1:2, 0:1]
    for half in range(2):
        span = slice(half * LANES, half * LANES + LANES)
        for axis, (pair, line) in enumerate(((0, 0), (0, 2), (1, 0))):
            rows[axis, span] = as_rows(atoms[own_block, pair, line + half : line + half + 1, :])
        kind = as_rows(atoms[own_block, 1, 2 + half : 3 + half, :])
        width = jnp.where(kind > 0.5, broad, narrow)
        rows[3, span] = lax.rsqrt(width * width + narrow * narrow)
        rows[4, span] = lax.rsqrt(width * width + broad * broad)


def build_piece(atoms, rows, piece):
    def one_block(block, carry):
        for half in range(2):
            x, y, z, kind = (
                jnp.broadcast_to(atoms[block, pair, line + half : line + half + 1, :], (8, LANES))
                for pair, line in ((0, 0), (0, 2), (1, 0), (1, 2))
            )
            second = kind > 0.5
            for group in range(GROUPS):
                span = slice(group * 8, group * 8 + 8)
                delta_x = rows[0, span] - x
                delta_y = rows[1, span] - y
                delta_z = rows[2, span] - z
                squared = delta_x * delta_x + delta_y * delta_y + delta_z * delta_z
                inverse = lax.rsqrt(squared)
                scale = jnp.where(second, rows[4, span], rows[3, span])
                piece[2 * block + half, span, :] = lax.erf(squared * inverse * scale) * inverse
        return carry

    lax.fori_loop(0, BLKS, one_block, 0, unroll=8)


def build_own_kernel(atoms, constants, piece, rows):
    _, own_block, _ = place_of()
    fill_rows(atoms, own_block, constants, rows)
    build_piece(atoms, rows, piece)
    width_0, width_1, hardness_0, hardness_1 = (constants[line : line + 1, 0:1] for line in range(4))
    for half in range(2):
        span = slice(half * LANES, half * LANES + LANES)
        second = as_rows(atoms[own_block, 1, 2 + half : 3 + half, :]) > 0.5
        diagonal = jnp.where(second, hardness_1, hardness_0) + inv_sqrt_pi / jnp.where(second, width_1, width_0)
        tile = piece[2 * own_block + half, span, :]
        piece[2 * own_block + half, span, :] = jnp.where(eye(LANES), diagonal, tile)


def apply_rows(pieces, direction, rep):
    sums = tuple(jnp.zeros((8, LANES), float32) for _ in range(GROUPS))
    for turn, piece in enumerate(pieces):
        for core in range(2):
            first = row_of(rep ^ turn, core * BLKS)

            def one_line(line, sums, core=core, piece=piece, first=first):
                values = jnp.broadcast_to(direction[pl.ds(first + line, 1), :], (8, LANES))
                here = core * BLKS + line
                return tuple(
                    sums[group] + piece[here, group * 8 : group * 8 + 8, :] * values for group in range(GROUPS)
                )

            sums = lax.fori_loop(0, BLKS, one_line, sums, unroll=16)
    half = GROUPS // 2
    return [
        jnp.sum(jnp.concatenate(sums[part * half : part * half + half], axis=0).T, axis=0, keepdims=True)
        for part in range(2)
    ]


def write_message(image, message):
    block = jnp.concatenate(image * 4, axis=0)
    for line in range(ROWS // 8):
        message[line * 8 : line * 8 + 8, :] = block


def project(vector, groups):
    members = ROWS * LANES // FRAGS
    taken = jnp.zeros_like(vector)
    for group in range(FRAGS):
        inside = groups == float(group)
        mean = total_of(jnp.where(inside, vector, 0.0)) / members
        taken = jnp.where(inside, mean, taken)
    return vector - taken


def build_kernel(part_1, rows, piece_1):
    build_piece(part_1, rows, piece_1)


def first_kernel(*refs):
    parts, (rows, own_piece, piece_1, piece_3, piece_2) = refs[:4], refs[4:9]
    message, residual, groups, norm = refs[9:]
    rep, _, _ = place_of()
    build_piece(parts[3], rows, piece_3)
    build_piece(parts[2], rows, piece_2)
    for turn, part in enumerate(parts):
        source = rep ^ turn
        for block in range(BLKS):
            lines = pl.ds(row_of(source, block * 2), 2)
            residual[lines, :] = part[block, 2, 0:2, :]
            groups[lines, :] = part[block, 2, 2:4, :]
    start = -project(residual[...], groups[...])
    residual[...] = start
    norm[...] = jnp.broadcast_to(total_of(start * start), norm.shape)
    write_message(apply_rows((own_piece, piece_1, piece_2, piece_3), residual, rep), message)


def update(image, residual, direction, charges, groups, norm, residual_out, direction_out, charges_out):
    norm_now = norm[0:1, 0:1]
    along, whole = direction[...], image[...]
    step = norm_now / total_of(along * whole)
    charges_out[...] = step * along if charges is None else charges[...] + step * along
    left = residual[...] - step * project(whole, groups[...])
    residual_out[...] = left
    norm_next = total_of(left * left)
    direction_out[...] = left + norm_next / norm_now * along
    return norm_next


def iterate_kernel(*refs, begun):
    image, residual, direction = refs[:3]
    charges = refs[3] if begun else None
    groups, norm, *pieces = refs[3 + begun : 9 + begun]
    message, residual_out, direction_out, charges_out, norm_out = refs[9 + begun :]
    norm_next = update(image, residual, direction, charges, groups, norm, residual_out, direction_out, charges_out)
    norm_out[...] = jnp.broadcast_to(norm_next, norm_out.shape)
    write_message(apply_rows(pieces, direction_out, place_of()[0]), message)


def last_kernel(
    image, residual, direction, charges, groups, norm, own, piece_1, piece_2, piece_3, share, message, *scratch
):
    residual_out, direction_out, charges_out = scratch
    rep, own_block, window = place_of()
    norm_next = update(image, residual, direction, charges, groups, norm, residual_out, direction_out, charges_out)
    applied = apply_rows((own, piece_1, piece_2, piece_3), direction_out, rep)
    line = row_of(rep, own_block * 2)
    part = applied[0] * direction_out[pl.ds(line, 1), :] + applied[1] * direction_out[pl.ds(line + 1, 1), :]
    share[...] = jnp.broadcast_to(jnp.sum(part, axis=1, keepdims=True) / norm_next, share.shape)
    for core in range(2):
        lines = pl.ds(row_of(rep, core * BLKS) + lax.rem(window // 2, 2), BLKS // 2, stride=2)
        half = slice(core * BLKS // 2, core * BLKS // 2 + BLKS // 2)
        message[half, :] = jnp.where(window < 4, charges_out[lines, :], direction_out[lines, :])


def join_kernel(shares, message, out):
    _, _, window = place_of()
    lane = lax.broadcasted_iota(jnp.int32, message.shape, 1)
    out[...] = jnp.where(lane // WINDOW == lax.rem(window, 2), message[...], total_of(shares[:, 0:1]))


def finish_kernel(
    parts, features, kinds, layer_in, layer_charge, layer_bias, layer_mid, layer_out, charges_out, energies_out
):
    frame = lax.axis_index("phase")
    inputs = [
        jnp.dot(layer_in[:, kind, :], features[frame], precision=highest, preferred_element_type=float32)
        + as_column(layer_bias[kind : kind + 1, :])
        for kind in range(ELEMS)
    ]
    block = parts[...]
    lane = lax.broadcasted_iota(jnp.int32, block.shape, 1) // WINDOW
    place = lax.broadcasted_iota(jnp.int32, block.shape, 0)
    solved = place // 4 % 4 == lax.rem(frame + 2, 4)
    sender = place // 16 * 4 + place % 4
    inside = lane == sender % 2
    lines = [
        jnp.sum(jnp.where(inside & solved & (sender // 2 == line), block, 0.0), axis=0, keepdims=True)
        for line in range(4)
    ]
    step = LANES - WINDOW
    step = step / total_of(jnp.where(solved & ~inside, block, 0.0))
    charges = jnp.concatenate([lines[0] + step * lines[2], lines[1] + step * lines[3]], axis=1)
    charges_out[...] = charges
    outs = []
    for kind in range(ELEMS):
        hidden_one = jnp.tanh(inputs[kind] + as_column(layer_charge[kind : kind + 1, :]) * charges)
        outs.append(last_layers(layer_mid, layer_out, hidden_one, kind))
    own = pl.ds(pl.multiple_of(lax.axis_index("rep") * OWN, OWN), OWN)
    energies_out[...] = jnp.where(kinds[pl.ds(frame, 1), own] == 1, outs[1], outs[0])


def call(kernel, outs, name, scratch=(), flops=0, held=VMEM):
    def run(*args):
        many = isinstance(outs, list)
        return pl.pallas_call(
            kernel,
            out_shape=outs,
            in_specs=[held] * len(args),
            out_specs=[VMEM] * len(outs) if many else VMEM,
            scratch_shapes=list(scratch),
            compiler_params=PARAMS,
            cost_estimate=pl.CostEstimate(flops=flops, bytes_accessed=0, transcendentals=0) if flops else None,
            name=name,
        )(*args)

    return run


def on_device(
    descriptors,
    positions,
    elements,
    fragments,
    neg_input,
    neg_bias,
    neg_hidden,
    neg_output,
    short_input,
    short_charge,
    short_bias,
    short_hidden,
    short_output,
    widths,
    hardness,
):
    all_axes = ("phase", "zq", "zr", "core", "rep")
    piece = pltpu.VMEM((PIECE, OWN, LANES), float32)
    rows = pltpu.VMEM((5, OWN, LANES), float32)
    whole = shaped(ROWS, LANES)
    small = shaped(8, LANES)

    def exchange(message):
        sent = message.reshape(ROWS // 2, 2, LANES)
        return lax.all_to_all(sent, all_axes, 0, 0, axis_index_groups=cube_groups()).reshape(ROWS, LANES)

    def kept(pieces):
        return [pltpu.with_memory_space_constraint(one, pltpu.VMEM) for one in pieces]

    def turned(layer):
        return jnp.transpose(layer, (1, 0, 2))

    given = [descriptors, turned(positions), elements, fragments, turned(neg_input), neg_bias, turned(neg_hidden)]
    given += [neg_output, widths[None, :], hardness[None, :]]
    held = [pltpu.VMEM(one.shape, one.dtype) for one in given]
    held[1] = pltpu.VMEM((3, elements.shape[0], OWN), float32)
    held[2] = pltpu.VMEM((elements.shape[0], OWN), jnp.int32)
    message, constants = call(
        prepare_kernel,
        [shaped(BLKS, 3, 4, LANES), small],
        "prepare",
        held + [pltpu.SemaphoreType.DMA((len(given),))],
        held=pl.BlockSpec(memory_space=pl.ANY),
    )(*[pltpu.with_memory_space_constraint(one, pltpu.HBM) for one in given])
    atoms_own = lax.all_to_all(message, all_axes, 0, 0, axis_index_groups=block_groups())
    parts = [
        lax.ppermute(atoms_own, "rep", [(rep ^ turn, rep) for rep in range(REPS)]) for turn in range(1, REPS)
    ]
    own_piece, row_values = call(build_own_kernel, [piece, rows], "build_own", flops=10**9)(atoms_own, constants)
    piece_1 = call(build_kernel, piece, "build_next", flops=10**9)(parts[0], *kept([row_values]))
    piece_3, piece_2, message, residual, groups, norm = call(
        first_kernel, [piece, piece, whole, whole, whole, small], "build_rest_and_begin"
    )(atoms_own, *parts, *kept([row_values, own_piece, piece_1]))
    pieces = [own_piece, piece_1, piece_2, piece_3]
    message, residual, direction, charges, norm = call(
        functools.partial(iterate_kernel, begun=0), [whole, whole, whole, whole, small], "iterate"
    )(exchange(message), residual, residual, groups, norm, *kept(pieces))
    message, residual, direction, charges, norm = call(
        functools.partial(iterate_kernel, begun=1), [whole, whole, whole, whole, small], "iterate"
    )(exchange(message), residual, direction, charges, groups, norm, *kept(pieces))
    share, message = call(
        last_kernel, [shaped(16, LANES), shaped(BLKS, LANES)], "last", [pltpu.VMEM((ROWS, LANES), float32)] * 3
    )(exchange(message), residual, direction, charges, groups, norm, *kept(pieces))
    shares = lax.all_to_all(share.reshape(16, 1, LANES), all_axes, 0, 0, axis_index_groups=layer_groups())
    shares = shares.reshape(16, LANES)
    message = call(join_kernel, shaped(BLKS, LANES), "join")(shares, message)
    parts = lax.all_to_all(
        message.reshape(BLKS, 1, LANES), all_axes, 0, 0, axis_index_groups=block_groups()
    ).reshape(BLKS, LANES)
    return call(finish_kernel, [shaped(1, OWN), shaped(1, OWN)], "finish")(
        parts,
        descriptors,
        elements,
        turned(short_input),
        short_charge,
        short_bias,
        turned(short_hidden),
        short_output,
    )


def solution(mesh):
    split = Mesh(mesh.devices.reshape(4, 4, 4, 2, 4), ("phase", "zq", "zr", "core", "rep"))
    block_axes = ("zq", "zr", "core")
    return jax.shard_map(
        on_device,
        mesh=split,
        in_specs=(
            P(None, None, block_axes + ("rep",)),
            P(None, None, block_axes),
            P(None, block_axes),
            P(None, block_axes + ("rep",)),
        )
        + (P(),) * 11,
        out_specs=(P("phase", block_axes + ("rep",)), P("phase", block_axes + ("rep",))),
        check_vma=False,
    )
```

```python
import functools

import jax
import jax.numpy as jnp
import numpy as np
from jax import lax
from jax.experimental import pallas as pl
from jax.experimental.pallas import tpu as pltpu
from jax.sharding import Mesh
from jax.sharding import PartitionSpec as P


FRAGS = 4
ELEMS = 2
LANES = 128
OWN = 256
REPS = 4
BLKS = 32
GROUPS = OWN // 8
PIECE = BLKS * 2
ROWS = REPS * PIECE
WINDOW = 64

highest = lax.Precision.HIGHEST
inv_sqrt_pi = 0.5641895835477563
float32 = jnp.float32
VMEM = pl.BlockSpec(memory_space=pltpu.VMEM)
SMEM = pl.BlockSpec(memory_space=pltpu.SMEM)
PARAMS = pltpu.CompilerParams(vmem_limit_bytes=12 * 2**20)


def shaped(*shape):
    return jax.ShapeDtypeStruct(shape, float32)


def eye(size):
    return lax.broadcasted_iota(jnp.int32, (size, size), 0) == lax.broadcasted_iota(jnp.int32, (size, size), 1)


def as_column(row):
    return jnp.sum(jnp.where(eye(row.shape[1]), row, 0.0), axis=1, keepdims=True)


def as_rows(row):
    return jnp.broadcast_to(row, (LANES, LANES)).T


def total_of(values):
    return jnp.sum(jnp.sum(values, axis=0, keepdims=True), axis=1, keepdims=True)


def last_layers(layer_mid, layer_out, hidden_one, kind):
    hidden_two = jnp.dot(layer_mid[:, kind, :], hidden_one, precision=highest, preferred_element_type=float32)
    return jnp.sum(as_column(layer_out[kind : kind + 1, :]) * jnp.tanh(hidden_two), axis=0, keepdims=True)


def network(layer_in, layer_bias, layer_mid, layer_out, features):
    outs = []
    for kind in range(ELEMS):
        hidden_one = jnp.dot(layer_in[:, kind, :], features, precision=highest, preferred_element_type=float32)
        hidden_one = jnp.tanh(hidden_one + as_column(layer_bias[kind : kind + 1, :]))
        outs.append(last_layers(layer_mid, layer_out, hidden_one, kind))
    return outs


def place_of():
    core, spot = lax.axis_index("core"), lax.axis_index("zr")
    turned = jnp.where(lax.axis_index("zq") < 2, 3 - spot, spot)
    return lax.axis_index("rep"), core * 16 + lax.rem(lax.axis_index("phase") + 2, 4) * 4 + turned, core * 4 + spot


def source_of(rep, turn):
    return rep ^ turn if turn in (0, 2) else rep ^ jnp.where(lax.axis_index("core") == 0, turn, 4 - turn)


def row_of(rep, line):
    return line // 32 * 128 + lax.rem(rep + 2, 4) * 32 + line % 32


def all_devices():
    return np.arange(512).reshape(4, 4, 4, 2, 4)[[2, 3, 0, 1]][..., [2, 3, 0, 1]]


def listed(groups):
    return [[int(device) for device in group] for group in groups]


def cube_groups():
    devices = all_devices()
    devices[:, :2] = devices[:, :2, ::-1].copy()
    return listed(devices.transpose(1, 3, 4, 0, 2).reshape(4, 128))


def block_groups():
    return listed(all_devices()[:, [2, 3, 0, 1]].transpose(0, 4, 3, 1, 2).reshape(16, BLKS))


def layer_groups():
    return listed(all_devices().transpose(1, 2, 3, 0, 4).reshape(BLKS, 16))


def prepare_kernel(*refs):
    given, (message, constants), held, arrived = refs[:10], refs[10:12], refs[12:22], refs[22]
    own = pl.ds(pl.multiple_of(lax.axis_index("rep") * OWN, OWN), OWN)
    copies = []
    for index, (source, target) in enumerate(zip(given, held)):
        source = source.at[:, :, own] if index == 1 else source.at[:, own] if index == 2 else source
        copies.append(pltpu.make_async_copy(source, target, arrived.at[index]))
        copies[-1].start()
    features, coords, kinds, groups, layer_in, layer_bias, layer_mid, layer_out, widths, hardness = held
    frames = features.shape[0]

    def send(frame, pair, one, two):
        block = jnp.concatenate([one[:, :LANES], one[:, LANES:], two[:, :LANES], two[:, LANES:]], axis=0)
        for target in range(BLKS // frames):
            message[target // 4 * 16 + (frame + 2) % 4 * 4 + target % 4, pair] = block

    for copy in copies[1:]:
        copy.wait()
    for frame in range(frames):
        send(frame, 0, coords[0, frame : frame + 1, :], coords[1, frame : frame + 1, :])
        send(frame, 1, coords[2, frame : frame + 1, :], kinds[frame : frame + 1, :].astype(float32))
    for line, source in enumerate((widths, hardness)):
        for kind in range(ELEMS):
            row = jnp.broadcast_to(source[0:1, kind : kind + 1], (1, LANES))
            constants[2 * line + kind : 2 * line + kind + 1, :] = row
    copies[0].wait()
    wide = jnp.concatenate([features[frame] for frame in range(frames)], axis=1)
    first, second = network(layer_in, layer_bias, layer_mid, layer_out, wide)
    for frame in range(frames):
        span = slice(frame * OWN, frame * OWN + OWN)
        electroneg = jnp.where(kinds[frame : frame + 1, :] == 1, second[:, span], first[:, span])
        send(frame, 2, electroneg, groups[frame : frame + 1, :].astype(float32))


def fill_rows(atoms, own_block, constants, rows):
    narrow, broad = constants[0:1, 0:1], constants[1:2, 0:1]
    for half in range(2):
        span = slice(half * LANES, half * LANES + LANES)
        for axis, (pair, line) in enumerate(((0, 0), (0, 2), (1, 0))):
            rows[axis, span] = as_rows(atoms[own_block, pair, line + half : line + half + 1, :])
        kind = as_rows(atoms[own_block, 1, 2 + half : 3 + half, :])
        width = jnp.where(kind > 0.5, broad, narrow)
        rows[3, span] = lax.rsqrt(width * width + narrow * narrow)
        rows[4, span] = lax.rsqrt(width * width + broad * broad)


def build_piece(atoms, rows, piece):
    def one_block(block, carry):
        for half in range(2):
            x, y, z, kind = (
                jnp.broadcast_to(atoms[block, pair, line + half : line + half + 1, :], (8, LANES))
                for pair, line in ((0, 0), (0, 2), (1, 0), (1, 2))
            )
            second = kind > 0.5
            for group in range(GROUPS):
                span = slice(group * 8, group * 8 + 8)
                delta_x = rows[0, span] - x
                delta_y = rows[1, span] - y
                delta_z = rows[2, span] - z
                squared = delta_x * delta_x + delta_y * delta_y + delta_z * delta_z
                inverse = lax.rsqrt(squared)
                scale = jnp.where(second, rows[4, span], rows[3, span])
                piece[2 * block + half, span, :] = lax.erf(squared * inverse * scale) * inverse
        return carry

    lax.fori_loop(0, BLKS, one_block, 0, unroll=8)


def build_own_kernel(atoms, constants, piece, rows):
    _, own_block, _ = place_of()
    fill_rows(atoms, own_block, constants, rows)
    build_piece(atoms, rows, piece)
    width_0, width_1, hardness_0, hardness_1 = (constants[line : line + 1, 0:1] for line in range(4))
    for half in range(2):
        span = slice(half * LANES, half * LANES + LANES)
        second = as_rows(atoms[own_block, 1, 2 + half : 3 + half, :]) > 0.5
        diagonal = jnp.where(second, hardness_1, hardness_0) + inv_sqrt_pi / jnp.where(second, width_1, width_0)
        tile = piece[2 * own_block + half, span, :]
        piece[2 * own_block + half, span, :] = jnp.where(eye(LANES), diagonal, tile)


def apply_rows(pieces, direction, rep):
    sums = tuple(jnp.zeros((8, LANES), float32) for _ in range(GROUPS))
    for turn, piece in enumerate(pieces):
        for core in range(2):
            first = row_of(source_of(rep, turn), core * BLKS)

            def one_line(line, sums, core=core, piece=piece, first=first):
                values = jnp.broadcast_to(direction[pl.ds(first + line, 1), :], (8, LANES))
                here = core * BLKS + line
                return tuple(
                    sums[group] + piece[here, group * 8 : group * 8 + 8, :] * values for group in range(GROUPS)
                )

            sums = lax.fori_loop(0, BLKS, one_line, sums, unroll=16)
    half = GROUPS // 2
    return [
        jnp.sum(jnp.concatenate(sums[part * half : part * half + half], axis=0).T, axis=0, keepdims=True)
        for part in range(2)
    ]


def write_message(image, message):
    block = jnp.concatenate(image * 4, axis=0)
    for line in range(ROWS // 8):
        message[line * 8 : line * 8 + 8, :] = block


def project(vector, groups):
    members = ROWS * LANES // FRAGS
    taken = jnp.zeros_like(vector)
    for group in range(FRAGS):
        inside = groups == float(group)
        mean = total_of(jnp.where(inside, vector, 0.0)) / members
        taken = jnp.where(inside, mean, taken)
    return vector - taken


def build_kernel(part_1, rows, piece_1):
    build_piece(part_1, rows, piece_1)


def first_kernel(*refs):
    parts, (rows, own_piece, piece_1, piece_3, piece_2) = refs[:4], refs[4:9]
    message, residual, groups, norm = refs[9:]
    rep, _, _ = place_of()
    build_piece(parts[3], rows, piece_3)
    build_piece(parts[2], rows, piece_2)
    for turn, part in enumerate(parts):
        source = source_of(rep, turn)
        for block in range(BLKS):
            lines = pl.ds(row_of(source, block * 2), 2)
            residual[lines, :] = part[block, 2, 0:2, :]
            groups[lines, :] = part[block, 2, 2:4, :]
    start = -project(residual[...], groups[...])
    residual[...] = start
    norm[...] = jnp.broadcast_to(total_of(start * start), norm.shape)
    write_message(apply_rows((own_piece, piece_1, piece_2, piece_3), residual, rep), message)


def update(image, residual, direction, charges, groups, norm, residual_out, direction_out, charges_out):
    norm_now = norm[0:1, 0:1]
    along, whole = direction[...], image[...]
    step = norm_now / total_of(along * whole)
    charges_out[...] = step * along if charges is None else charges[...] + step * along
    left = residual[...] - step * project(whole, groups[...])
    residual_out[...] = left
    norm_next = total_of(left * left)
    direction_out[...] = left + norm_next / norm_now * along
    return norm_next


def iterate_kernel(*refs, begun):
    image, residual, direction = refs[:3]
    charges = refs[3] if begun else None
    groups, norm, *pieces = refs[3 + begun : 9 + begun]
    message, residual_out, direction_out, charges_out, norm_out = refs[9 + begun :]
    norm_next = update(image, residual, direction, charges, groups, norm, residual_out, direction_out, charges_out)
    norm_out[...] = jnp.broadcast_to(norm_next, norm_out.shape)
    write_message(apply_rows(pieces, direction_out, place_of()[0]), message)


def last_kernel(
    image, residual, direction, charges, groups, norm, own, piece_1, piece_2, piece_3, share, message, *scratch
):
    residual_out, direction_out, charges_out = scratch
    rep, own_block, window = place_of()
    norm_next = update(image, residual, direction, charges, groups, norm, residual_out, direction_out, charges_out)
    applied = apply_rows((own, piece_1, piece_2, piece_3), direction_out, rep)
    line = row_of(rep, own_block * 2)
    part = applied[0] * direction_out[pl.ds(line, 1), :] + applied[1] * direction_out[pl.ds(line + 1, 1), :]
    share[...] = jnp.broadcast_to(jnp.sum(part, axis=1, keepdims=True) / norm_next, share.shape)
    for core in range(2):
        lines = pl.ds(row_of(rep, core * BLKS) + lax.rem(window // 2, 2), BLKS // 2, stride=2)
        half = slice(core * BLKS // 2, core * BLKS // 2 + BLKS // 2)
        message[half, :] = jnp.where(window < 4, charges_out[lines, :], direction_out[lines, :])


def join_kernel(shares, message, out):
    _, _, window = place_of()
    lane = lax.broadcasted_iota(jnp.int32, message.shape, 1)
    out[...] = jnp.where(lane // WINDOW == lax.rem(window, 2), message[...], total_of(shares[:, 0:1]))


def finish_kernel(
    parts, features, kinds, layer_in, layer_charge, layer_bias, layer_mid, layer_out, charges_out, energies_out
):
    frame = lax.axis_index("phase")
    inputs = [
        jnp.dot(layer_in[:, kind, :], features[frame], precision=highest, preferred_element_type=float32)
        + as_column(layer_bias[kind : kind + 1, :])
        for kind in range(ELEMS)
    ]
    block = parts[...]
    lane = lax.broadcasted_iota(jnp.int32, block.shape, 1) // WINDOW
    place = lax.broadcasted_iota(jnp.int32, block.shape, 0)
    solved = place // 4 % 4 == lax.rem(frame + 2, 4)
    sender = place // 16 * 4 + place % 4
    inside = lane == sender % 2
    lines = [
        jnp.sum(jnp.where(inside & solved & (sender // 2 == line), block, 0.0), axis=0, keepdims=True)
        for line in range(4)
    ]
    step = LANES - WINDOW
    step = step / total_of(jnp.where(solved & ~inside, block, 0.0))
    charges = jnp.concatenate([lines[0] + step * lines[2], lines[1] + step * lines[3]], axis=1)
    charges_out[...] = charges
    outs = []
    for kind in range(ELEMS):
        hidden_one = jnp.tanh(inputs[kind] + as_column(layer_charge[kind : kind + 1, :]) * charges)
        outs.append(last_layers(layer_mid, layer_out, hidden_one, kind))
    own = pl.ds(pl.multiple_of(lax.axis_index("rep") * OWN, OWN), OWN)
    energies_out[...] = jnp.where(kinds[pl.ds(frame, 1), own] == 1, outs[1], outs[0])


def call(kernel, outs, name, scratch=(), flops=0, held=VMEM):
    def run(*args):
        many = isinstance(outs, list)
        return pl.pallas_call(
            kernel,
            out_shape=outs,
            in_specs=[held] * len(args),
            out_specs=[VMEM] * len(outs) if many else VMEM,
            scratch_shapes=list(scratch),
            compiler_params=PARAMS,
            cost_estimate=pl.CostEstimate(flops=flops, bytes_accessed=0, transcendentals=0) if flops else None,
            name=name,
        )(*args)

    return run


def on_device(
    descriptors,
    positions,
    elements,
    fragments,
    neg_input,
    neg_bias,
    neg_hidden,
    neg_output,
    short_input,
    short_charge,
    short_bias,
    short_hidden,
    short_output,
    widths,
    hardness,
):
    all_axes = ("phase", "zq", "zr", "core", "rep")
    piece = pltpu.VMEM((PIECE, OWN, LANES), float32)
    rows = pltpu.VMEM((5, OWN, LANES), float32)
    whole = shaped(ROWS, LANES)
    small = shaped(8, LANES)

    def exchange(message):
        sent = message.reshape(ROWS // 2, 2, LANES)
        return lax.all_to_all(sent, all_axes, 0, 0, axis_index_groups=cube_groups()).reshape(ROWS, LANES)

    def kept(pieces):
        return [pltpu.with_memory_space_constraint(one, pltpu.VMEM) for one in pieces]

    def turned(layer):
        return jnp.transpose(layer, (1, 0, 2))

    given = [descriptors, turned(positions), elements, fragments, turned(neg_input), neg_bias, turned(neg_hidden)]
    given += [neg_output, widths[None, :], hardness[None, :]]
    held = [pltpu.VMEM(one.shape, one.dtype) for one in given]
    held[1] = pltpu.VMEM((3, elements.shape[0], OWN), float32)
    held[2] = pltpu.VMEM((elements.shape[0], OWN), jnp.int32)
    message, constants = call(
        prepare_kernel,
        [shaped(BLKS, 3, 4, LANES), small],
        "prepare",
        held + [pltpu.SemaphoreType.DMA((len(given),))],
        held=pl.BlockSpec(memory_space=pl.ANY),
    )(*[pltpu.with_memory_space_constraint(one, pltpu.HBM) for one in given])
    atoms_own = lax.all_to_all(message, all_axes, 0, 0, axis_index_groups=block_groups())
    far = [(core * REPS + (rep ^ turn), core * REPS + rep) for core, turn in ((0, 1), (1, 3)) for rep in range(REPS)]
    part_1 = lax.ppermute(atoms_own, ("core", "rep"), far)
    part_2 = lax.ppermute(atoms_own, "rep", [(rep ^ 2, rep) for rep in range(REPS)])
    own_piece, row_values = call(build_own_kernel, [piece, rows], "build_own", flops=10**9)(atoms_own, constants)
    part_1, row_values = lax.optimization_barrier((part_1, row_values))
    part_3 = lax.ppermute(part_1, "core", [(0, 1), (1, 0)])
    parts = [part_1, part_2, part_3]
    piece_1 = call(build_kernel, piece, "build_next", flops=10**9)(part_1, *kept([row_values]))
    piece_3, piece_2, message, residual, groups, norm = call(
        first_kernel, [piece, piece, whole, whole, whole, small], "build_rest_and_begin"
    )(atoms_own, *parts, *kept([row_values, own_piece, piece_1]))
    pieces = [own_piece, piece_1, piece_2, piece_3]
    message, residual, direction, charges, norm = call(
        functools.partial(iterate_kernel, begun=0), [whole, whole, whole, whole, small], "iterate"
    )(exchange(message), residual, residual, groups, norm, *kept(pieces))
    message, residual, direction, charges, norm = call(
        functools.partial(iterate_kernel, begun=1), [whole, whole, whole, whole, small], "iterate"
    )(exchange(message), residual, direction, charges, groups, norm, *kept(pieces))
    share, message = call(
        last_kernel, [shaped(16, LANES), shaped(BLKS, LANES)], "last", [pltpu.VMEM((ROWS, LANES), float32)] * 3
    )(exchange(message), residual, direction, charges, groups, norm, *kept(pieces))
    shares = lax.all_to_all(share.reshape(16, 1, LANES), all_axes, 0, 0, axis_index_groups=layer_groups())
    shares = shares.reshape(16, LANES)
    message = call(join_kernel, shaped(BLKS, LANES), "join")(shares, message)
    parts = lax.all_to_all(
        message.reshape(BLKS, 1, LANES), all_axes, 0, 0, axis_index_groups=block_groups()
    ).reshape(BLKS, LANES)
    return call(finish_kernel, [shaped(1, OWN), shaped(1, OWN)], "finish")(
        parts,
        descriptors,
        elements,
        turned(short_input),
        short_charge,
        short_bias,
        turned(short_hidden),
        short_output,
    )


def solution(mesh):
    split = Mesh(mesh.devices.reshape(4, 4, 4, 2, 4), ("phase", "zq", "zr", "core", "rep"))
    block_axes = ("zq", "zr", "core")
    return jax.shard_map(
        on_device,
        mesh=split,
        in_specs=(
            P(None, None, block_axes + ("rep",)),
            P(None, None, block_axes),
            P(None, block_axes),
            P(None, block_axes + ("rep",)),
        )
        + (P(),) * 11,
        out_specs=(P("phase", block_axes + ("rep",)), P("phase", block_axes + ("rep",))),
        check_vma=False,
    )
```

```python
import functools

import jax
import jax.numpy as jnp
import numpy as np
from jax import lax
from jax.experimental import pallas as pl
from jax.experimental.pallas import tpu as pltpu
from jax.sharding import Mesh
from jax.sharding import PartitionSpec as P


FRAGS = 4
ELEMS = 2
LANES = 128
OWN = 256
REPS = 4
BLKS = 32
GROUPS = OWN // 8
PIECE = BLKS * 2
ROWS = REPS * PIECE
WINDOW = 64

precise = lax.Precision.HIGH
inv_sqrt_pi = 0.5641895835477563
float32 = jnp.float32
VMEM = pl.BlockSpec(memory_space=pltpu.VMEM)
SMEM = pl.BlockSpec(memory_space=pltpu.SMEM)
PARAMS = pltpu.CompilerParams(vmem_limit_bytes=12 * 2**20)


def shaped(*shape):
    return jax.ShapeDtypeStruct(shape, float32)


def eye(size):
    return lax.broadcasted_iota(jnp.int32, (size, size), 0) == lax.broadcasted_iota(jnp.int32, (size, size), 1)


def as_column(row):
    return jnp.sum(jnp.where(eye(row.shape[1]), row, 0.0), axis=1, keepdims=True)


def as_rows(row):
    return jnp.broadcast_to(row, (LANES, LANES)).T


def total_of(values):
    return jnp.sum(jnp.sum(values, axis=0, keepdims=True), axis=1, keepdims=True)


def last_layers(layer_mid, layer_out, hidden_one, kind):
    hidden_two = jnp.dot(layer_mid[:, kind, :], hidden_one, precision=precise, preferred_element_type=float32)
    return jnp.sum(as_column(layer_out[kind : kind + 1, :]) * jnp.tanh(hidden_two), axis=0, keepdims=True)


def network(layer_in, layer_bias, layer_mid, layer_out, features):
    outs = []
    for kind in range(ELEMS):
        hidden_one = jnp.dot(layer_in[:, kind, :], features, precision=precise, preferred_element_type=float32)
        hidden_one = jnp.tanh(hidden_one + as_column(layer_bias[kind : kind + 1, :]))
        outs.append(last_layers(layer_mid, layer_out, hidden_one, kind))
    return outs


def place_of():
    core, spot = lax.axis_index("core"), lax.axis_index("zr")
    turned = jnp.where(lax.axis_index("zq") < 2, 3 - spot, spot)
    return lax.axis_index("rep"), core * 16 + lax.rem(lax.axis_index("phase") + 2, 4) * 4 + turned, core * 4 + spot


def source_of(rep, turn):
    return rep ^ turn if turn in (0, 2) else rep ^ jnp.where(lax.axis_index("core") == 0, turn, 4 - turn)


def row_of(rep, line):
    return line // 32 * 128 + lax.rem(rep + 2, 4) * 32 + line % 32


def all_devices():
    return np.arange(512).reshape(4, 4, 4, 2, 4)[[2, 3, 0, 1]][..., [2, 3, 0, 1]]


def listed(groups):
    return [[int(device) for device in group] for group in groups]


def cube_groups():
    devices = all_devices()
    devices[:, :2] = devices[:, :2, ::-1].copy()
    return listed(devices.transpose(1, 3, 4, 0, 2).reshape(4, 128))


def block_groups():
    return listed(all_devices()[:, [2, 3, 0, 1]].transpose(0, 4, 3, 1, 2).reshape(16, BLKS))


def layer_groups():
    return listed(all_devices().transpose(1, 2, 3, 0, 4).reshape(BLKS, 16))


def prepare_kernel(*refs):
    given, (message, constants), held, arrived = refs[:10], refs[10:12], refs[12:22], refs[22]
    own = pl.ds(pl.multiple_of(lax.axis_index("rep") * OWN, OWN), OWN)
    copies = []
    for index, (source, target) in enumerate(zip(given, held)):
        source = source.at[:, :, own] if index == 1 else source.at[:, own] if index == 2 else source
        copies.append(pltpu.make_async_copy(source, target, arrived.at[index]))
        copies[-1].start()
    features, coords, kinds, groups, layer_in, layer_bias, layer_mid, layer_out, widths, hardness = held
    frames = features.shape[0]

    def send(frame, pair, one, two):
        block = jnp.concatenate([one[:, :LANES], one[:, LANES:], two[:, :LANES], two[:, LANES:]], axis=0)
        for target in range(BLKS // frames):
            message[target // 4 * 16 + (frame + 2) % 4 * 4 + target % 4, pair] = block

    for copy in copies[1:]:
        copy.wait()
    for frame in range(frames):
        send(frame, 0, coords[0, frame : frame + 1, :], coords[1, frame : frame + 1, :])
        send(frame, 1, coords[2, frame : frame + 1, :], kinds[frame : frame + 1, :].astype(float32))
    for line, source in enumerate((widths, hardness)):
        for kind in range(ELEMS):
            row = jnp.broadcast_to(source[0:1, kind : kind + 1], (1, LANES))
            constants[2 * line + kind : 2 * line + kind + 1, :] = row
    copies[0].wait()
    wide = jnp.concatenate([features[frame] for frame in range(frames)], axis=1)
    first, second = network(layer_in, layer_bias, layer_mid, layer_out, wide)
    for frame in range(frames):
        span = slice(frame * OWN, frame * OWN + OWN)
        electroneg = jnp.where(kinds[frame : frame + 1, :] == 1, second[:, span], first[:, span])
        send(frame, 2, electroneg, groups[frame : frame + 1, :].astype(float32))


def fill_rows(atoms, own_block, constants, rows):
    narrow, broad = constants[0:1, 0:1], constants[1:2, 0:1]
    for half in range(2):
        span = slice(half * LANES, half * LANES + LANES)
        for axis, (pair, line) in enumerate(((0, 0), (0, 2), (1, 0))):
            rows[axis, span] = as_rows(atoms[own_block, pair, line + half : line + half + 1, :])
        kind = as_rows(atoms[own_block, 1, 2 + half : 3 + half, :])
        width = jnp.where(kind > 0.5, broad, narrow)
        rows[3, span] = lax.rsqrt(width * width + narrow * narrow)
        rows[4, span] = lax.rsqrt(width * width + broad * broad)


def build_piece(atoms, rows, piece):
    def one_block(block, carry):
        for half in range(2):
            x, y, z, kind = (
                jnp.broadcast_to(atoms[block, pair, line + half : line + half + 1, :], (8, LANES))
                for pair, line in ((0, 0), (0, 2), (1, 0), (1, 2))
            )
            second = kind > 0.5
            for group in range(GROUPS):
                span = slice(group * 8, group * 8 + 8)
                delta_x = rows[0, span] - x
                delta_y = rows[1, span] - y
                delta_z = rows[2, span] - z
                squared = delta_x * delta_x + delta_y * delta_y + delta_z * delta_z
                inverse = lax.rsqrt(squared)
                scale = jnp.where(second, rows[4, span], rows[3, span])
                piece[2 * block + half, span, :] = lax.erf(squared * inverse * scale) * inverse
        return carry

    lax.fori_loop(0, BLKS, one_block, 0, unroll=8)


def build_own_kernel(atoms, constants, piece, rows):
    _, own_block, _ = place_of()
    fill_rows(atoms, own_block, constants, rows)
    build_piece(atoms, rows, piece)
    width_0, width_1, hardness_0, hardness_1 = (constants[line : line + 1, 0:1] for line in range(4))
    for half in range(2):
        span = slice(half * LANES, half * LANES + LANES)
        second = as_rows(atoms[own_block, 1, 2 + half : 3 + half, :]) > 0.5
        diagonal = jnp.where(second, hardness_1, hardness_0) + inv_sqrt_pi / jnp.where(second, width_1, width_0)
        tile = piece[2 * own_block + half, span, :]
        piece[2 * own_block + half, span, :] = jnp.where(eye(LANES), diagonal, tile)


def apply_rows(pieces, direction, rep):
    sums = tuple(jnp.zeros((8, LANES), float32) for _ in range(GROUPS))
    for turn, piece in enumerate(pieces):
        for core in range(2):
            first = row_of(source_of(rep, turn), core * BLKS)

            def one_line(line, sums, core=core, piece=piece, first=first):
                values = jnp.broadcast_to(direction[pl.ds(first + line, 1), :], (8, LANES))
                here = core * BLKS + line
                return tuple(
                    sums[group] + piece[here, group * 8 : group * 8 + 8, :] * values for group in range(GROUPS)
                )

            sums = lax.fori_loop(0, BLKS, one_line, sums, unroll=32)
    half = GROUPS // 2
    return [
        jnp.sum(jnp.concatenate(sums[part * half : part * half + half], axis=0).T, axis=0, keepdims=True)
        for part in range(2)
    ]


def write_message(image, message):
    block = jnp.concatenate(image * 4, axis=0)
    for line in range(ROWS // 8):
        message[line * 8 : line * 8 + 8, :] = block


def project(vector, groups):
    members = ROWS * LANES // FRAGS
    taken = jnp.zeros_like(vector)
    for group in range(FRAGS):
        inside = groups == float(group)
        mean = total_of(jnp.where(inside, vector, 0.0)) / members
        taken = jnp.where(inside, mean, taken)
    return vector - taken


def build_kernel(part_1, rows, piece_1):
    build_piece(part_1, rows, piece_1)


def first_kernel(*refs):
    parts, (rows, own_piece, piece_1, piece_3, piece_2) = refs[:4], refs[4:9]
    message, residual, groups, norm = refs[9:]
    rep, _, _ = place_of()
    build_piece(parts[3], rows, piece_3)
    build_piece(parts[2], rows, piece_2)
    for turn, part in enumerate(parts):
        source = source_of(rep, turn)
        for block in range(BLKS):
            lines = pl.ds(row_of(source, block * 2), 2)
            residual[lines, :] = part[block, 2, 0:2, :]
            groups[lines, :] = part[block, 2, 2:4, :]
    start = -project(residual[...], groups[...])
    residual[...] = start
    norm[...] = jnp.broadcast_to(total_of(start * start), norm.shape)
    write_message(apply_rows((own_piece, piece_1, piece_2, piece_3), residual, rep), message)


def update(image, residual, direction, charges, groups, norm, residual_out, direction_out, charges_out):
    norm_now = norm[0:1, 0:1]
    along, whole = direction[...], image[...]
    step = norm_now / total_of(along * whole)
    charges_out[...] = step * along if charges is None else charges[...] + step * along
    left = residual[...] - step * project(whole, groups[...])
    residual_out[...] = left
    norm_next = total_of(left * left)
    direction_out[...] = left + norm_next / norm_now * along
    return norm_next


def iterate_kernel(*refs, begun):
    image, residual, direction = refs[:3]
    charges = refs[3] if begun else None
    groups, norm, *pieces = refs[3 + begun : 9 + begun]
    message, residual_out, direction_out, charges_out, norm_out = refs[9 + begun :]
    norm_next = update(image, residual, direction, charges, groups, norm, residual_out, direction_out, charges_out)
    norm_out[...] = jnp.broadcast_to(norm_next, norm_out.shape)
    write_message(apply_rows(pieces, direction_out, place_of()[0]), message)


def last_kernel(
    image, residual, direction, charges, groups, norm, own, piece_1, piece_2, piece_3, share, message, *scratch
):
    residual_out, direction_out, charges_out = scratch
    rep, own_block, window = place_of()
    norm_next = update(image, residual, direction, charges, groups, norm, residual_out, direction_out, charges_out)
    applied = apply_rows((own, piece_1, piece_2, piece_3), direction_out, rep)
    line = row_of(rep, own_block * 2)
    part = applied[0] * direction_out[pl.ds(line, 1), :] + applied[1] * direction_out[pl.ds(line + 1, 1), :]
    share[...] = jnp.broadcast_to(jnp.sum(part, axis=1, keepdims=True) / norm_next, share.shape)
    for core in range(2):
        lines = pl.ds(row_of(rep, core * BLKS) + lax.rem(window // 2, 2), BLKS // 2, stride=2)
        half = slice(core * BLKS // 2, core * BLKS // 2 + BLKS // 2)
        message[half, :] = jnp.where(window < 4, charges_out[lines, :], direction_out[lines, :])


def join_kernel(shares, message, out):
    _, _, window = place_of()
    lane = lax.broadcasted_iota(jnp.int32, message.shape, 1)
    out[...] = jnp.where(lane // WINDOW == lax.rem(window, 2), message[...], total_of(shares[:, 0:1]))


def finish_kernel(
    parts, features, kinds, layer_in, layer_charge, layer_bias, layer_mid, layer_out, charges_out, energies_out
):
    frame = lax.axis_index("phase")
    inputs = [
        jnp.dot(layer_in[:, kind, :], features[frame], precision=precise, preferred_element_type=float32)
        + as_column(layer_bias[kind : kind + 1, :])
        for kind in range(ELEMS)
    ]
    block = parts[...]
    lane = lax.broadcasted_iota(jnp.int32, block.shape, 1) // WINDOW
    place = lax.broadcasted_iota(jnp.int32, block.shape, 0)
    solved = place // 4 % 4 == lax.rem(frame + 2, 4)
    sender = place // 16 * 4 + place % 4
    inside = lane == sender % 2
    lines = [
        jnp.sum(jnp.where(inside & solved & (sender // 2 == line), block, 0.0), axis=0, keepdims=True)
        for line in range(4)
    ]
    step = LANES - WINDOW
    step = step / total_of(jnp.where(solved & ~inside, block, 0.0))
    charges = jnp.concatenate([lines[0] + step * lines[2], lines[1] + step * lines[3]], axis=1)
    charges_out[...] = charges
    outs = []
    for kind in range(ELEMS):
        hidden_one = jnp.tanh(inputs[kind] + as_column(layer_charge[kind : kind + 1, :]) * charges)
        outs.append(last_layers(layer_mid, layer_out, hidden_one, kind))
    own = pl.ds(pl.multiple_of(lax.axis_index("rep") * OWN, OWN), OWN)
    energies_out[...] = jnp.where(kinds[pl.ds(frame, 1), own] == 1, outs[1], outs[0])


def call(kernel, outs, name, scratch=(), flops=0, held=VMEM):
    def run(*args):
        many = isinstance(outs, list)
        return pl.pallas_call(
            kernel,
            out_shape=outs,
            in_specs=[held] * len(args),
            out_specs=[VMEM] * len(outs) if many else VMEM,
            scratch_shapes=list(scratch),
            compiler_params=PARAMS,
            cost_estimate=pl.CostEstimate(flops=flops, bytes_accessed=0, transcendentals=0) if flops else None,
            name=name,
        )(*args)

    return run


def on_device(
    descriptors,
    positions,
    elements,
    fragments,
    neg_input,
    neg_bias,
    neg_hidden,
    neg_output,
    short_input,
    short_charge,
    short_bias,
    short_hidden,
    short_output,
    widths,
    hardness,
):
    all_axes = ("phase", "zq", "zr", "core", "rep")
    piece = pltpu.VMEM((PIECE, OWN, LANES), float32)
    rows = pltpu.VMEM((5, OWN, LANES), float32)
    whole = shaped(ROWS, LANES)
    small = shaped(8, LANES)

    def exchange(message):
        sent = message.reshape(ROWS // 2, 2, LANES)
        return lax.all_to_all(sent, all_axes, 0, 0, axis_index_groups=cube_groups()).reshape(ROWS, LANES)

    def kept(pieces):
        return [pltpu.with_memory_space_constraint(one, pltpu.VMEM) for one in pieces]

    def turned(layer):
        return jnp.transpose(layer, (1, 0, 2))

    given = [descriptors, turned(positions), elements, fragments, turned(neg_input), neg_bias, turned(neg_hidden)]
    given += [neg_output, widths[None, :], hardness[None, :]]
    held = [pltpu.VMEM(one.shape, one.dtype) for one in given]
    held[1] = pltpu.VMEM((3, elements.shape[0], OWN), float32)
    held[2] = pltpu.VMEM((elements.shape[0], OWN), jnp.int32)
    message, constants = call(
        prepare_kernel,
        [shaped(BLKS, 3, 4, LANES), small],
        "prepare",
        held + [pltpu.SemaphoreType.DMA((len(given),))],
        held=pl.BlockSpec(memory_space=pl.ANY),
    )(*[pltpu.with_memory_space_constraint(one, pltpu.HBM) for one in given])
    atoms_own = lax.all_to_all(message, all_axes, 0, 0, axis_index_groups=block_groups())
    far = [(core * REPS + (rep ^ turn), core * REPS + rep) for core, turn in ((0, 1), (1, 3)) for rep in range(REPS)]
    part_1 = lax.ppermute(atoms_own, ("core", "rep"), far)
    part_2 = lax.ppermute(atoms_own, "rep", [(rep ^ 2, rep) for rep in range(REPS)])
    own_piece, row_values = call(build_own_kernel, [piece, rows], "build_own", flops=10**9)(atoms_own, constants)
    part_1, row_values = lax.optimization_barrier((part_1, row_values))
    part_3 = lax.ppermute(part_1, "core", [(0, 1), (1, 0)])
    parts = [part_1, part_2, part_3]
    piece_1 = call(build_kernel, piece, "build_next", flops=10**9)(part_1, *kept([row_values]))
    piece_3, piece_2, message, residual, groups, norm = call(
        first_kernel, [piece, piece, whole, whole, whole, small], "build_rest_and_begin"
    )(atoms_own, *parts, *kept([row_values, own_piece, piece_1]))
    pieces = [own_piece, piece_1, piece_2, piece_3]
    message, residual, direction, charges, norm = call(
        functools.partial(iterate_kernel, begun=0), [whole, whole, whole, whole, small], "iterate"
    )(exchange(message), residual, residual, groups, norm, *kept(pieces))
    message, residual, direction, charges, norm = call(
        functools.partial(iterate_kernel, begun=1), [whole, whole, whole, whole, small], "iterate"
    )(exchange(message), residual, direction, charges, groups, norm, *kept(pieces))
    share, message = call(
        last_kernel, [shaped(16, LANES), shaped(BLKS, LANES)], "last", [pltpu.VMEM((ROWS, LANES), float32)] * 3
    )(exchange(message), residual, direction, charges, groups, norm, *kept(pieces))
    shares = lax.all_to_all(share.reshape(16, 1, LANES), all_axes, 0, 0, axis_index_groups=layer_groups())
    shares = shares.reshape(16, LANES)
    message = call(join_kernel, shaped(BLKS, LANES), "join")(shares, message)
    parts = lax.all_to_all(
        message.reshape(BLKS, 1, LANES), all_axes, 0, 0, axis_index_groups=block_groups()
    ).reshape(BLKS, LANES)
    return call(finish_kernel, [shaped(1, OWN), shaped(1, OWN)], "finish")(
        parts,
        descriptors,
        elements,
        turned(short_input),
        short_charge,
        short_bias,
        turned(short_hidden),
        short_output,
    )


def solution(mesh):
    split = Mesh(mesh.devices.reshape(4, 4, 4, 2, 4), ("phase", "zq", "zr", "core", "rep"))
    block_axes = ("zq", "zr", "core")
    return jax.shard_map(
        on_device,
        mesh=split,
        in_specs=(
            P(None, None, block_axes + ("rep",)),
            P(None, None, block_axes),
            P(None, block_axes),
            P(None, block_axes + ("rep",)),
        )
        + (P(),) * 11,
        out_specs=(P("phase", block_axes + ("rep",)), P("phase", block_axes + ("rep",))),
        check_vma=False,
    )
```
